256 devices in a mesh: ctx: 32 (over y, x, core), tp: 8 (over z).
Axes of the slice: x: 4, y: 4, z: 8, core: 2. Of those that a mesh axis runs over, the one named last changes fastest.
Arguments:
- x_raw: bfloat16 [49152, 8192], P('ctx', 'tp'), may hold values from -6 to 6
- bc_raw: bfloat16 [49152, 256], P('ctx'), may hold values from -6 to 6
- z_gate: bfloat16 [49152, 8192], P('ctx', 'tp'), may hold values from -6 to 6
- conv_x: float32 [4, 8192], P(None, 'tp'), may hold values from -3 to 3
- conv_bc: float32 [4, 256], replicated, may hold values from -3 to 3
- step_size: float32 [49152, 128], P('ctx', 'tp'), may hold values from 0.0007 to 0.063, as said below
- log_decay: float32 [49152, 128], P('ctx', 'tp'), may hold values from -0.62 to 0, as said below
- skip_scale: float32 [128], P('tp'), may hold values from 0.5 to 3, as said below
- norm_gain: float32 [8192], P('tp'), may hold values from 0.5 to 1.5
Outputs:
- layer_out: bfloat16 [49152, 8192], P('ctx', 'tp')
The draws below stay inside these ranges and needn't reach their ends.
Inputs may be any that keep to these rules, and one draw needn't show every extreme that they name: `step_size`: positive step sizes. `log_decay`: each entry is negative; exp of it is the factor by which the head's state is kept from the previous token. `skip_scale`: positive coefficients.
All inputs are finite; a program needn't handle non-finite values.
Results may differ from the reference program's by a relative error of at most 0.0065.
Values may be sent and summed in bfloat16 or wider, within the bound.
A program may use at most 192 MiB of HBM per device.

```python
import jax
import jax.numpy as jnp
from jax import lax

SSM_HEAD_COUNT = 128
HEAD_DIM = 64
STATE = 128
CONV = 4
BLOCK_LEN = 256
TOK_DEV = 1536
TOKEN_COUNT = 49152


def slow_heads_of(key, slow_share):
    return jax.random.bernoulli(jax.random.fold_in(key, 101), slow_share, (SSM_HEAD_COUNT,))


def draw_log_decay(key, part):
    slow_heads = slow_heads_of(key, 0.55)
    key = jax.random.fold_in(key, 3)
    random_key_parts = jax.random.split(key, 6)
    slow_rate = jnp.exp(jax.random.uniform(random_key_parts[0], (SSM_HEAD_COUNT,), jnp.float32, jnp.log(0.05), jnp.log(0.3))) / TOKEN_COUNT
    fast_rate = jnp.exp(jax.random.uniform(random_key_parts[1], (SSM_HEAD_COUNT,), jnp.float32, jnp.log(1.0 / 50.0), jnp.log(1.0 / 30.0)))
    decay_speed = jnp.where(slow_heads, slow_rate, fast_rate)
    device_multiplier = jnp.exp(jax.random.uniform(random_key_parts[2], (TOKEN_COUNT // TOK_DEV, SSM_HEAD_COUNT), jnp.float32, jnp.log(0.5), jnp.log(2.0)))
    device_multiplier = jnp.repeat(device_multiplier, TOK_DEV, axis=0)
    jaggedness = jax.random.uniform(random_key_parts[3], (TOKEN_COUNT, SSM_HEAD_COUNT), jnp.float32, 0.5, 1.5)
    spike_positions = jax.random.randint(random_key_parts[4], (3,), 0, TOKEN_COUNT)
    spike_rows = jnp.any(jnp.arange(TOKEN_COUNT)[:, None] == spike_positions[None, :], axis=1)
    spike_penalty = jax.random.uniform(random_key_parts[5], (TOKEN_COUNT, SSM_HEAD_COUNT), jnp.float32, 0.22, 0.51)
    return -(decay_speed[None, :] * device_multiplier * jaggedness) - jnp.where(spike_rows[:, None], spike_penalty, 0.0)


def draw_step_size(key, part):
    slow_heads = slow_heads_of(key, 0.55)
    key = jax.random.fold_in(key, 5)
    random_key_parts = jax.random.split(key, 2)
    step_base = jnp.where(slow_heads, 0.002, 0.03) * jnp.exp(jax.random.uniform(random_key_parts[0], (SSM_HEAD_COUNT,), jnp.float32, jnp.log(0.7), jnp.log(1.4)))
    jaggedness = jax.random.uniform(random_key_parts[1], (TOKEN_COUNT, SSM_HEAD_COUNT), jnp.float32, 0.5, 1.5)
    return step_base[None, :] * jaggedness


def skip_values(key, growth):
    spread = jax.random.uniform(key, (SSM_HEAD_COUNT,), jnp.float32, 0.5, 1.0)
    return spread * growth ** (jnp.arange(SSM_HEAD_COUNT).astype(jnp.float32) / SSM_HEAD_COUNT)


def draw_skip_scale(key, part):
    key = jax.random.fold_in(key, 7)
    return skip_values(key, 2.0)


def block_scale(rng, dims, cuts, smallest, top_value):
    level, own = 1.0, jax.random.fold_in(rng, 6)
    for axis_at, parts in cuts:
        steps = jnp.exp(jax.random.uniform(jax.random.fold_in(own, axis_at), (parts,), jnp.float32, smallest / len(cuts), top_value / len(cuts)))
        level = level * jnp.repeat(steps, dims[axis_at] // parts).reshape([-1 if axis == axis_at else 1 for axis in range(len(dims))])
    return level


def gaussian(stream_key, shape, deviation, bound, cuts=(), kind=jnp.bfloat16):
    entries = jax.random.normal(stream_key, shape, jnp.float32) * deviation
    if len(cuts) > 0:
        entries = block_scale(stream_key, shape, cuts, -0.22, 0.18) * entries
    return jnp.clip(entries, min=-bound, max=bound).astype(kind)


def setup_inputs(seed: int = 0) -> dict:
    streams_of = jax.random.split(jax.random.key(seed), 10)
    x_raw = gaussian(streams_of[0], (TOKEN_COUNT, SSM_HEAD_COUNT * HEAD_DIM), 1.0, 6.0, ((0, 32), (1, 8)))
    bc_raw = gaussian(streams_of[1], (TOKEN_COUNT, 2 * STATE), 1.0, 6.0, ((0, 32),))
    z_gate = gaussian(streams_of[2], (TOKEN_COUNT, SSM_HEAD_COUNT * HEAD_DIM), 1.0, 6.0, ((0, 32), (1, 8)))
    conv_x = gaussian(streams_of[3], (CONV, SSM_HEAD_COUNT * HEAD_DIM), CONV ** -0.5, 3.0, ((1, 8),), jnp.float32)
    conv_bc = gaussian(streams_of[4], (CONV, 2 * STATE), CONV ** -0.5, 3.0, (), jnp.float32)
    step_size = draw_step_size(jax.random.fold_in(streams_of[9], 71), 0)
    log_decay = draw_log_decay(jax.random.fold_in(streams_of[9], 71), 0)
    skip_scale = draw_skip_scale(jax.random.fold_in(streams_of[9], 71), 0)
    norm_gain = jnp.clip(1.0 + 0.1 * jax.random.normal(streams_of[8], (SSM_HEAD_COUNT * HEAD_DIM,), jnp.float32), 0.5, 1.5)
    return {"x_raw": x_raw, "bc_raw": bc_raw, "z_gate": z_gate, "conv_x": conv_x, "conv_bc": conv_bc, "step_size": step_size, "log_decay": log_decay, "skip_scale": skip_scale, "norm_gain": norm_gain}


def causal_conv(padded, taps_weight, length):
    tap_count = taps_weight.shape[0]
    summed = jnp.zeros((length, taps_weight.shape[1]), jnp.float32)
    for tap_index in range(tap_count):
        summed = summed + taps_weight[tap_index] * padded[tap_index:tap_index + length].astype(jnp.float32)
    return jax.nn.silu(summed).astype(jnp.bfloat16)

def block_pass(state_in, inputs, b_rows, c_rows, step_rows, log_rows):
    count = log_rows.shape[0]
    running = jnp.cumsum(log_rows, axis=0)
    scores = jnp.dot(c_rows, b_rows.T, preferred_element_type=jnp.float32)
    decay_gaps = running.T[:, :, None] - running.T[:, None, :]
    positions = jnp.arange(count)
    causal = positions[:, None] >= positions[None, :]
    decay_matrix = jnp.where(causal[None], jnp.exp(jnp.where(causal[None], decay_gaps, 0.0)), 0.0)
    weights = (scores[None] * decay_matrix * step_rows.T[:, None, :]).astype(jnp.bfloat16)
    inner_out = jnp.einsum('hts,shp->thp', weights.astype(jnp.float32), inputs.astype(jnp.float32))
    block_total = running[-1]
    scaled = ((jnp.exp(block_total[None, :] - running) * step_rows)[:, :, None] * inputs.astype(jnp.float32)).astype(jnp.bfloat16)
    block_state = jnp.einsum('shp,sn->hpn', scaled.astype(jnp.float32), b_rows.astype(jnp.float32))
    carried = jnp.exp(running)[:, :, None] * jnp.einsum('tn,hpn->thp', c_rows.astype(jnp.float32), state_in, precision=lax.Precision.HIGHEST)
    new_state = jnp.exp(block_total)[:, None, None] * state_in + block_state
    return (new_state, inner_out + carried)

def reference(x_raw, bc_raw, z_gate, conv_x, conv_bc, step_size, log_decay, skip_scale, norm_gain):
    tap_count = conv_x.shape[0]
    x_conv = causal_conv(jnp.pad(x_raw, ((tap_count - 1, 0), (0, 0))), conv_x, TOKEN_COUNT)
    bc_conv = causal_conv(jnp.pad(bc_raw, ((tap_count - 1, 0), (0, 0))), conv_bc, TOKEN_COUNT)
    blocks = TOKEN_COUNT // BLOCK_LEN
    inputs = x_conv.reshape(blocks, BLOCK_LEN, SSM_HEAD_COUNT, HEAD_DIM)
    b_all = bc_conv[:, :STATE].reshape(blocks, BLOCK_LEN, STATE)
    c_all = bc_conv[:, STATE:].reshape(blocks, BLOCK_LEN, STATE)
    step_all = step_size.reshape(blocks, BLOCK_LEN, SSM_HEAD_COUNT)
    log_all = log_decay.reshape(blocks, BLOCK_LEN, SSM_HEAD_COUNT)
    gate_all = z_gate.reshape(blocks, BLOCK_LEN, SSM_HEAD_COUNT, HEAD_DIM)

    def one_block(state_in, pieces):
        inputs_b, b_rows, c_rows, step_rows, log_rows, gate_rows = pieces
        new_state, ssm_part = block_pass(state_in, inputs_b, b_rows, c_rows, step_rows, log_rows)
        ssm_out = ssm_part + skip_scale[None, :, None] * inputs_b.astype(jnp.float32)
        gated_out = (ssm_out * jax.nn.silu(gate_rows.astype(jnp.float32))).reshape(BLOCK_LEN, SSM_HEAD_COUNT * HEAD_DIM)
        mean_square = lax.optimization_barrier(jnp.mean(gated_out * gated_out, axis=1, keepdims=True))
        normed = (gated_out * lax.rsqrt(mean_square + 1e-05) * norm_gain[None, :]).astype(jnp.bfloat16)
        return (new_state, normed)
    empty_state = jnp.zeros((SSM_HEAD_COUNT, HEAD_DIM, STATE), jnp.float32)
    _, outputs = lax.scan(one_block, empty_state, (inputs, b_all, c_all, step_all, log_all, gate_all))
    return outputs.reshape(TOKEN_COUNT, SSM_HEAD_COUNT * HEAD_DIM)
```

```python
import functools

import jax
import jax.numpy as jnp
from jax import lax
from jax.experimental import pallas as pl
from jax.experimental.pallas import tpu as pltpu
from jax.sharding import PartitionSpec as P

F32 = jnp.float32
BF16 = jnp.bfloat16
MESH = pl.DeviceIdType.MESH
CHUNK = 128
GROUP = 256
HALO = 16


def split2(value):
    high = value.astype(BF16)
    return high, (value - high.astype(F32)).astype(BF16)


def split3(value):
    high = value.astype(BF16)
    rest = value - high.astype(F32)
    mid = rest.astype(BF16)
    return high, mid, (rest - mid.astype(F32)).astype(BF16)


def silu(value):
    half = 0.5 * value
    return half * jnp.tanh(half) + half


def conv_silu(rows, taps):
    wide = rows.astype(F32)[8:]
    behind = pltpu.roll(wide, 1, 0)
    near = taps[3] * wide + taps[2] * behind
    far = taps[1] * wide + taps[0] * behind
    return silu((near + pltpu.roll(far, 2, 0))[8:])


def mixer(
    ctx_size, tp_size, head_dim,
    x_hbm, bc_hbm, z_hbm, convx_ref, convbc_ref, step_hbm, log_hbm, skip_ref,
    g_hbm, ssq_ref,
    xbuf, bcbuf, zbuf, stepbuf, logbuf, spread, tri, fin, fout, rowbuf, rows_ref,
    sc, bt, xconv, xs, state, parts, recv, lam_own, lam, lam_wide, send, start_state,
    local_ref, gate_ref, gbuf, ssq, ssq_recv,
    load_sem, halo_send, halo_recv, lam_send, lam_recv, part_send, part_recv,
    start_send, start_recv, ssq_send, ssq_recv_sem, out_sem,
):
    length, channels = x_hbm.shape
    heads = step_hbm.shape[1]
    chunks = length // CHUNK
    groups = channels // GROUP
    n_state = bt.shape[1]
    part_rows = parts.shape[1]
    per_group = ctx_size // groups
    mid = CHUNK // 2 - 1
    me = lax.axis_index("ctx")
    tp = lax.axis_index("tp")

    def cols(g):
        return slice(g * GROUP, (g + 1) * GROUP)

    loads = [
        pltpu.make_async_copy(log_hbm, logbuf, load_sem.at[0]),
        pltpu.make_async_copy(step_hbm, stepbuf, load_sem.at[1]),
        pltpu.make_async_copy(bc_hbm, bcbuf.at[pl.ds(HALO, length)], load_sem.at[2]),
    ]
    x_loads = [
        pltpu.make_async_copy(
            x_hbm.at[:, cols(g)], xbuf.at[pl.ds(HALO, length), cols(g)], load_sem.at[4 + g]
        )
        for g in range(groups)
    ]
    z_load = pltpu.make_async_copy(z_hbm, zbuf, load_sem.at[3])
    for load in loads + x_loads + [z_load]:
        load.start()

    barrier = pltpu.get_barrier_semaphore()

    def greet_ctx(k, _):
        pl.semaphore_signal(barrier, inc=1, device_id=(lax.rem(me + k, ctx_size), tp), device_id_type=MESH)
        return 0

    def greet_tp(k, _):
        pl.semaphore_signal(barrier, inc=1, device_id=(me, lax.rem(tp + k, tp_size)), device_id_type=MESH)
        return 0

    lax.fori_loop(1, ctx_size, greet_ctx, 0)
    lax.fori_loop(1, tp_size, greet_tp, 0)

    t_at = lax.broadcasted_iota(jnp.int32, (CHUNK, CHUNK), 0)
    s_at = lax.broadcasted_iota(jnp.int32, (CHUNK, CHUNK), 1)
    lower = jnp.where(t_at >= s_at, 1.0, 0.0).astype(BF16)
    for k in range(3):
        tri[:, k * CHUNK : (k + 1) * CHUNK] = lower
    head_at = lax.broadcasted_iota(jnp.int32, (heads, channels), 0)
    channel_at = lax.broadcasted_iota(jnp.int32, (heads, channels), 1)
    first = head_at * head_dim
    one_map = jnp.where((channel_at >= first) & (channel_at < first + head_dim), 1.0, 0.0).astype(BF16)
    for k in range(3):
        spread[k * heads : (k + 1) * heads, :] = one_map
    rowbuf[...] = jnp.zeros_like(rowbuf)

    loads[0].wait()
    loads[1].wait()
    low_lane = lax.broadcasted_iota(jnp.int32, (CHUNK, 2 * heads), 1) < heads

    def two_halves(value):
        high = value.astype(BF16).astype(F32)
        return jnp.where(low_lane, high, value - high).astype(BF16)

    def decays(c, carry):
        before, tail = carry
        at = pl.multiple_of(c * CHUNK, CHUNK)
        pieces = jnp.concatenate(split3(logbuf[pl.ds(at, CHUNK), :]), axis=0)
        running = jnp.dot(tri[...], pieces, preferred_element_type=F32)
        middle = running[mid : mid + 1]
        end = running[CHUNK - 1 : CHUNK]
        centred = running - middle
        centred = jnp.concatenate((centred, centred), axis=1)
        steps = stepbuf[pl.ds(at, CHUNK), :]
        steps = jnp.concatenate((steps, steps), axis=1)
        fin[pl.ds(at, CHUNK), :] = two_halves(jnp.exp(-centred) * steps)
        fout[pl.ds(at, CHUNK), :] = two_halves(jnp.exp(centred))
        rowbuf[pl.ds(c, 1), :] = jnp.exp(middle + tail)
        rowbuf[pl.ds(16 + c, 1), :] = jnp.exp(before + middle)
        return before + end, end - middle

    zero_row = jnp.zeros((1, heads), F32)
    total, tail = lax.fori_loop(0, chunks, decays, (zero_row, zero_row))
    rowbuf[chunks : chunks + 1, :] = jnp.exp(tail)
    rowbuf[30:31, :] = skip_ref[...]
    rows_ref[...] = jnp.dot(
        jnp.concatenate(split3(rowbuf[...]), axis=1), spread[...], preferred_element_type=F32
    )
    lam_own[...] = jnp.zeros_like(lam_own)
    lam_own[0:1, 0:heads] = jnp.exp(total)
    lam[me] = lam_own[...]

    pl.semaphore_wait(barrier, ctx_size + tp_size - 2)

    right = lax.rem(me + 1, ctx_size)
    x_halo = pltpu.make_async_remote_copy(
        src_ref=x_hbm.at[pl.ds(length - HALO, HALO)], dst_ref=xbuf.at[pl.ds(0, HALO)],
        send_sem=halo_send.at[0], recv_sem=halo_recv.at[0], device_id=(right, tp), device_id_type=MESH,
    )
    bc_halo = pltpu.make_async_remote_copy(
        src_ref=bc_hbm.at[pl.ds(length - HALO, HALO)], dst_ref=bcbuf.at[pl.ds(0, HALO)],
        send_sem=halo_send.at[1], recv_sem=halo_recv.at[1], device_id=(right, tp), device_id_type=MESH,
    )
    bc_halo.start()
    x_halo.start()

    def lam_copy(dst, src):
        return pltpu.make_async_remote_copy(
            src_ref=lam_own, dst_ref=lam.at[src], send_sem=lam_send.at[dst], recv_sem=lam_recv.at[src],
            device_id=(dst, tp), device_id_type=MESH,
        )

    def part_copy(dst, src):
        return pltpu.make_async_remote_copy(
            src_ref=parts.at[dst], dst_ref=recv.at[src], send_sem=part_send.at[dst],
            recv_sem=part_recv.at[src], device_id=(dst, tp), device_id_type=MESH,
        )

    def start_copy(dst, src):
        row = pl.multiple_of((src // groups) * part_rows, part_rows)
        return pltpu.make_async_remote_copy(
            src_ref=send.at[dst], dst_ref=start_state.at[lax.rem(src, groups), pl.ds(row, part_rows)],
            send_sem=start_send.at[dst], recv_sem=start_recv.at[src], device_id=(dst, tp), device_id_type=MESH,
        )

    def ssq_copy(dst, src):
        return pltpu.make_async_remote_copy(
            src_ref=ssq, dst_ref=ssq_recv.at[src], send_sem=ssq_send.at[dst],
            recv_sem=ssq_recv_sem.at[src], device_id=(me, dst), device_id_type=MESH,
        )

    def each_peer(fn):
        def step(k, _):
            fn(lax.rem(me + k, ctx_size))
            return 0

        lax.fori_loop(1, ctx_size, step, 0)

    def each_tp(fn):
        def step(k, _):
            fn(lax.rem(tp + k, tp_size))
            return 0

        lax.fori_loop(1, tp_size, step, 0)

    each_peer(lambda d: lam_copy(d, me).start())

    loads[2].wait()
    bc_taps = [convbc_ref[k : k + 1, :] for k in range(4)]

    def project(c):
        at = pl.multiple_of(c * CHUNK, CHUNK)
        both = conv_silu(bcbuf[pl.ds(at, CHUNK + HALO), :], bc_taps).astype(BF16)
        c_rows = both[:, n_state:]
        b_turned = both[:, :n_state].T
        bt[c] = b_turned
        scores = jnp.dot(c_rows, b_turned, preferred_element_type=F32)
        causal = lax.broadcasted_iota(jnp.int32, (CHUNK, CHUNK), 0) >= lax.broadcasted_iota(
            jnp.int32, (CHUNK, CHUNK), 1
        )
        sc[c, :, :CHUNK] = jnp.where(causal, scores, 0.0).astype(BF16)
        sc[c, :, CHUNK:] = c_rows

    def project_step(c, _):
        project(c)
        return 0

    lax.fori_loop(1, chunks, project_step, 0)
    bc_halo.wait_recv()
    x_halo.wait_recv()
    bcbuf[0:HALO, :] = jnp.where(me > 0, bcbuf[0:HALO, :].astype(F32), 0.0).astype(BF16)
    xbuf[0:HALO, :] = jnp.where(me > 0, xbuf[0:HALO, :].astype(F32), 0.0).astype(BF16)
    project(0)

    def carry_through():
        each_peer(lambda s: lam_copy(s, s).wait_recv())
        each_peer(lambda s: part_copy(s, s).wait_recv())
        col = pl.multiple_of(lax.rem(me, groups) * GROUP, GROUP)
        lam_wide[...] = jnp.dot(
            jnp.concatenate(split3(lam[:, 0, :heads]), axis=1), spread[:, pl.ds(col, GROUP)],
            preferred_element_type=F32,
        )

        def step(d, running):
            send[d] = running.astype(BF16)
            return lam_wide[pl.ds(d, 1), :] * running + recv[d].astype(F32)

        lax.fori_loop(0, ctx_size, step, jnp.zeros((part_rows, GROUP), F32), unroll=4)
        row = pl.multiple_of((me // groups) * part_rows, part_rows)
        start_state[lax.rem(me, groups), pl.ds(row, part_rows), :] = send[me]
        each_peer(lambda d: start_copy(d, me).start())

    for g in range(groups):
        x_loads[g].wait()
        taps = [convx_ref[k : k + 1, cols(g)] for k in range(4)]
        state[...] = jnp.zeros_like(state)

        def forward(c, _, g=g, taps=taps):
            at = pl.multiple_of(c * CHUNK, CHUNK)
            value = conv_silu(xbuf[pl.ds(at, CHUNK + HALO), cols(g)], taps)
            xconv[pl.ds(at, CHUNK), cols(g)] = value.astype(BF16)
            scale = jnp.dot(fin[pl.ds(at, CHUNK), :], spread[: 2 * heads, cols(g)], preferred_element_type=F32)
            scaled = (value * scale).astype(BF16)
            held = state[...]
            xs[c, :CHUNK, cols(g)] = scaled
            xs[c, CHUNK:, cols(g)] = held.astype(BF16)
            added = jnp.dot(bt[c], scaled, preferred_element_type=F32)
            state[...] = rows_ref[pl.ds(c + 1, 1), cols(g)] * (held + added)
            return 0

        lax.fori_loop(0, chunks, forward, 0)
        for r in range(per_group):
            parts[r * groups + g] = state[r * part_rows : (r + 1) * part_rows, :].astype(BF16)

        @pl.when(lax.rem(me, groups) == g)
        def _():
            recv[me] = parts[me]

        def send_part(k, _, g=g):
            dst = lax.rem(me // groups + k, per_group) * groups + g

            @pl.when(dst != me)
            def _():
                part_copy(dst, me).start()

            return 0

        lax.fori_loop(0, per_group, send_part, 0)
        if g > 0:
            pl.when(lax.rem(me, groups) == g - 1)(carry_through)

    z_load.wait()

    def local(c, _):
        at = pl.multiple_of(c * CHUNK, CHUNK)
        for g in range(groups):
            inner = jnp.dot(sc[c], xs[c, :, cols(g)], preferred_element_type=F32)
            scale = jnp.dot(fout[pl.ds(at, CHUNK), :], spread[: 2 * heads, cols(g)], preferred_element_type=F32)
            gate = silu(zbuf[pl.ds(at, CHUNK), cols(g)].astype(F32))
            skipped = rows_ref[30:31, cols(g)] * xconv[pl.ds(at, CHUNK), cols(g)].astype(F32)
            local_ref[pl.ds(at, CHUNK), cols(g)] = (inner * scale + skipped) * gate
            gate_ref[pl.ds(at, CHUNK), cols(g)] = (
                scale * gate * rows_ref[pl.ds(16 + c, 1), cols(g)]
            ).astype(BF16)
        return 0

    lax.fori_loop(0, chunks // 2, local, 0)
    pl.when(lax.rem(me, groups) == groups - 1)(carry_through)
    lax.fori_loop(chunks // 2, chunks, local, 0)

    each_peer(lambda s: start_copy(s, s).wait_recv())
    ssq[...] = jnp.zeros_like(ssq)

    def out_copy(c):
        at = pl.multiple_of(c * CHUNK, CHUNK)
        return pltpu.make_async_copy(gbuf.at[pl.ds(at, CHUNK)], g_hbm.at[pl.ds(at, CHUNK)], out_sem.at[c])

    def finish(c, _):
        at = pl.multiple_of(c * CHUNK, CHUNK)
        squares = jnp.zeros((CHUNK, 128), F32)
        for g in range(groups):
            carried = jnp.dot(sc[c, :, CHUNK:], start_state[g], preferred_element_type=F32)
            gated = local_ref[pl.ds(at, CHUNK), cols(g)] + gate_ref[pl.ds(at, CHUNK), cols(g)].astype(F32) * carried
            gbuf[pl.ds(at, CHUNK), cols(g)] = gated.astype(BF16)
            both = gated * gated
            for lane in range(0, GROUP, 128):
                squares = squares + both[:, lane : lane + 128]
        ssq[pl.ds(c, 1), :] = jnp.sum(squares.T, axis=0, keepdims=True)
        out_copy(c).start()
        return 0

    lax.fori_loop(0, chunks, finish, 0)
    ssq_recv[tp] = ssq[...]
    each_tp(lambda d: ssq_copy(d, tp).start())

    bc_halo.wait_send()
    x_halo.wait_send()
    each_peer(lambda d: lam_copy(d, d).wait_send())
    each_peer(lambda d: part_copy(d, d).wait_send())
    each_peer(lambda d: start_copy(d, d).wait_send())
    each_tp(lambda s: ssq_copy(s, s).wait_recv())
    ssq_ref[...] = jnp.sum(ssq_recv[...], axis=0)
    each_tp(lambda d: ssq_copy(d, d).wait_send())

    def out_done(c, _):
        out_copy(c).wait()
        return 0

    lax.fori_loop(0, chunks, out_done, 0)


def norm(count, per_step, g_ref, ssq_ref, gain_ref, out_ref):
    for k in range(per_step):
        at = pl.program_id(0) * per_step + k
        row = lax.rsqrt(ssq_ref[pl.ds(at, 1), :] * (1.0 / count) + 1e-5)
        column = jnp.broadcast_to(row, (CHUNK, CHUNK)).T
        for lane in range(0, g_ref.shape[1], 128):
            here = (slice(k * CHUNK, (k + 1) * CHUNK), slice(lane, lane + 128))
            out_ref[here] = (g_ref[here].astype(F32) * column * gain_ref[:, lane : lane + 128]).astype(BF16)


def per_device(
    x_raw, bc_raw, z_gate, conv_x, conv_bc, step_size, log_decay, skip_scale, norm_gain, *, ctx_size, tp_size
):
    length, channels = x_raw.shape
    heads = step_size.shape[1]
    head_dim = channels // heads
    n_state = bc_raw.shape[1] // 2
    chunks = length // CHUNK
    groups = channels // GROUP
    part_rows = n_state * groups // ctx_size
    anywhere = pl.BlockSpec(memory_space=pl.ANY)
    in_vmem = pl.BlockSpec(memory_space=pltpu.VMEM)
    vmem = pltpu.VMEM
    dma = pltpu.SemaphoreType.DMA
    gated, squares = pl.pallas_call(
        functools.partial(mixer, ctx_size, tp_size, head_dim),
        out_shape=(
            jax.ShapeDtypeStruct((length, channels), BF16),
            jax.ShapeDtypeStruct((16, 128), F32),
        ),
        in_specs=[anywhere, anywhere, anywhere, in_vmem, in_vmem, anywhere, anywhere, in_vmem],
        out_specs=(anywhere, in_vmem),
        scratch_shapes=[
            vmem((length + HALO, channels), BF16),
            vmem((length + HALO, 2 * n_state), BF16),
            vmem((length, channels), BF16),
            vmem((length, heads), F32),
            vmem((length, heads), F32),
            vmem((3 * heads, channels), BF16),
            vmem((CHUNK, 3 * CHUNK), BF16),
            vmem((length, 2 * heads), BF16),
            vmem((length, 2 * heads), BF16),
            vmem((32, heads), F32),
            vmem((32, channels), F32),
            vmem((chunks, CHUNK, CHUNK + n_state), BF16),
            vmem((chunks, n_state, CHUNK), BF16),
            vmem((length, channels), BF16),
            vmem((chunks, CHUNK + n_state, channels), BF16),
            vmem((n_state, GROUP), F32),
            vmem((ctx_size, part_rows, GROUP), BF16),
            vmem((ctx_size, part_rows, GROUP), BF16),
            vmem((8, 128), F32),
            vmem((ctx_size, 8, 128), F32),
            vmem((ctx_size, GROUP), F32),
            vmem((ctx_size, part_rows, GROUP), BF16),
            vmem((groups, n_state, GROUP), BF16),
            vmem((length, channels), F32),
            vmem((length, channels), BF16),
            vmem((length, channels), BF16),
            vmem((16, 128), F32),
            vmem((tp_size, 16, 128), F32),
            dma((4 + groups,)),
            dma((2,)),
            dma((2,)),
            dma((ctx_size,)),
            dma((ctx_size,)),
            dma((ctx_size,)),
            dma((ctx_size,)),
            dma((ctx_size,)),
            dma((ctx_size,)),
            dma((tp_size,)),
            dma((tp_size,)),
            dma((chunks,)),
        ],
        compiler_params=pltpu.CompilerParams(
            collective_id=0, has_side_effects=True, vmem_limit_bytes=44 * 1024 * 1024
        ),
        name="mixer",
    )(x_raw, bc_raw, z_gate, conv_x, conv_bc, step_size, log_decay, skip_scale.reshape(1, heads))

    per_step = 2
    return pl.pallas_call(
        functools.partial(norm, channels * tp_size, per_step),
        grid=(chunks // per_step,),
        out_shape=jax.ShapeDtypeStruct((length, channels), BF16),
        in_specs=[
            pl.BlockSpec((per_step * CHUNK, channels), lambda i: (i, 0)),
            pl.BlockSpec((16, 128), lambda i: (0, 0)),
            pl.BlockSpec((1, channels), lambda i: (0, 0)),
        ],
        out_specs=pl.BlockSpec((per_step * CHUNK, channels), lambda i: (i, 0)),
        name="norm",
    )(gated, squares, norm_gain.reshape(1, channels))


def solution(mesh):
    sizes = dict(mesh.shape)
    return jax.shard_map(
        functools.partial(per_device, ctx_size=sizes["ctx"], tp_size=sizes["tp"]),
        mesh=mesh,
        in_specs=(
            P("ctx", "tp"),
            P("ctx", None),
            P("ctx", "tp"),
            P(None, "tp"),
            P(),
            P("ctx", "tp"),
            P("ctx", "tp"),
            P("tp"),
            P("tp"),
        ),
        out_specs=P("ctx", "tp"),
        check_vma=False,
    )
```

```python
import functools

import jax
import jax.numpy as jnp
from jax import lax
from jax.experimental import pallas as pl
from jax.experimental.pallas import tpu as pltpu
from jax.sharding import PartitionSpec as P

F32 = jnp.float32
BF16 = jnp.bfloat16
MESH = pl.DeviceIdType.MESH
CHUNK = 128
LANES = 128
GROUP = 256
TILES = GROUP // LANES
HALO = 16
BATCH = 4
PAIR = 2


def split3(value):
    high = value.astype(BF16)
    rest = value - high.astype(F32)
    mid = rest.astype(BF16)
    return high, mid, (rest - mid.astype(F32)).astype(BF16)


def silu_of_half(half):
    return half * jnp.tanh(half) + half


def dot(left, right):
    return jnp.dot(left, right, preferred_element_type=F32)


def mixer(
    ctx_size, tp_size, head_dim,
    x_hbm, bc_hbm, z_hbm, convx_hbm, convbc_hbm, step_hbm, log_hbm, skip_hbm, gain_hbm,
    out_hbm,
    xbuf, bcbuf, zbuf, stepbuf, logbuf, convx_ref, convbc_ref, skip_ref, gain_ref,
    spread, factor_map, shift_one, shift_all, shift_rim, sums, factors, rows_ref,
    scores_ref, c_ref, bt, xconv, xs, state, parts, recv, lam_wide, send, start_state,
    ahead, local_ref, gate_ref, squares, ssq, ssq_recv, inverse,
    load_sem, halo_send, halo_recv, part_send, part_recv, start_send, start_recv, ssq_send, ssq_recv_sem,
    out_sem,
):
    length, channels = x_hbm.shape
    heads = step_hbm.shape[0]
    chunks = length // CHUNK
    groups = channels // GROUP
    n_state = bt.shape[1]
    part_rows = parts.shape[2]
    per_group = ctx_size // groups
    mid = CHUNK // 2 - 1
    me = lax.axis_index("ctx")
    tp = lax.axis_index("tp")
    mine = lax.rem(me, groups)
    my_row = pl.multiple_of((me // groups) * part_rows, part_rows)

    def wide(ref, g, *at):
        return jnp.concatenate([ref[(g * TILES + k, *at)] for k in range(TILES)], axis=-1)

    def put(ref, g, at, value):
        for k in range(TILES):
            ref[(g * TILES + k, *at)] = value[:, k * LANES : (k + 1) * LANES]

    def rows_of(c):
        return pl.ds(pl.multiple_of(c * CHUNK, CHUNK), CHUNK)

    small_loads = [
        pltpu.make_async_copy(src, dst, load_sem.at[k])
        for k, (src, dst) in enumerate(
            (
                (log_hbm, logbuf),
                (step_hbm, stepbuf),
                (skip_hbm, skip_ref),
                (convbc_hbm, convbc_ref),
                (convx_hbm, convx_ref),
                (gain_hbm, gain_ref),
            )
        )
    ]
    bc_loads = [
        pltpu.make_async_copy(
            bc_hbm.at[:, pl.ds(k * LANES, LANES)], bcbuf.at[k, pl.ds(HALO, length)], load_sem.at[6 + k]
        )
        for k in range(2)
    ]

    def x_load(k):
        col = pl.ds(pl.multiple_of(k * LANES, LANES), LANES)
        return pltpu.make_async_copy(x_hbm.at[:, col], xbuf.at[k, pl.ds(HALO, length)], load_sem.at[8 + k])

    def z_load(k):
        col = pl.ds(pl.multiple_of(k * LANES, LANES), LANES)
        return pltpu.make_async_copy(
            z_hbm.at[:, col], zbuf.at[k], load_sem.at[8 + groups * TILES + k]
        )

    for load in small_loads + bc_loads:
        load.start()
    for k in range(groups * TILES):
        x_load(k).start()
    for k in range(groups * TILES):
        z_load(k).start()

    barrier = pltpu.get_barrier_semaphore()

    def greet_ctx(k, _):
        pl.semaphore_signal(barrier, inc=1, device_id=(lax.rem(me + k, ctx_size), tp), device_id_type=MESH)
        return 0

    def greet_tp(k, _):
        pl.semaphore_signal(barrier, inc=1, device_id=(me, lax.rem(tp + k, tp_size)), device_id_type=MESH)
        return 0

    lax.fori_loop(1, ctx_size, greet_ctx, 0)
    lax.fori_loop(1, tp_size, greet_tp, 0)

    s_at = lax.broadcasted_iota(jnp.int32, (CHUNK, CHUNK), 0)
    t_at = lax.broadcasted_iota(jnp.int32, (CHUNK, CHUNK), 1)
    upto = jnp.where(s_at <= t_at, 1.0, 0.0)
    sums[0] = (upto - jnp.where(s_at <= mid, 1.0, 0.0)).astype(BF16)
    sums[1] = upto.astype(BF16)
    sums[2] = jnp.ones((CHUNK, CHUNK), BF16)

    head_at = lax.broadcasted_iota(jnp.int32, (heads, channels), 0)
    channel_at = lax.broadcasted_iota(jnp.int32, (heads, channels), 1)
    first = head_at * head_dim
    one_map = jnp.where((channel_at >= first) & (channel_at < first + head_dim), 1.0, 0.0).astype(BF16)
    factor_map[...] = jnp.zeros_like(factor_map)
    for k in range(3):
        spread[k * heads : (k + 1) * heads, :] = one_map
        for term in range(2):
            row = (2 * k + term) * heads
            for lane in range(groups * TILES):
                factor_map[k, lane, row : row + heads, :] = one_map[:, lane * LANES : (lane + 1) * LANES]

    def shift(by, width, before):
        to = lax.broadcasted_iota(jnp.int32, (CHUNK, width), 0)
        at = lax.broadcasted_iota(jnp.int32, (CHUNK, width), 1)
        return jnp.where(to + (before - by) == at, 1.0, 0.0).astype(BF16)

    for by in range(4):
        shift_all[by] = shift(by, CHUNK, 0)
        if by > 0:
            shift_one[(by - 1) * CHUNK : by * CHUNK, :] = shift(by, CHUNK + HALO, HALO)
    halo_to = lax.broadcasted_iota(jnp.int32, (CHUNK, 3 * HALO), 0)
    halo_at = lax.broadcasted_iota(jnp.int32, (CHUNK, 3 * HALO), 1)
    halo_hit = halo_to < 0
    for by in range(1, 4):
        inside = (halo_at >= (by - 1) * HALO) & (halo_at < by * HALO)
        halo_hit = halo_hit | ((halo_to + (by * HALO - by) == halo_at) & inside)
    shift_rim[...] = jnp.where(halo_hit, 1.0, 0.0).astype(BF16)

    for load in small_loads:
        load.wait()

    def decays(b, carry):
        before, windows = carry
        batch = [b * BATCH + k for k in range(BATCH)]
        window = lax.broadcasted_iota(jnp.int32, (CHUNK, CHUNK), 1) * CHUNK + mid
        results = []
        for c in batch:
            pieces = jnp.concatenate(split3(logbuf[:, rows_of(c)]), axis=0)
            token = lax.broadcasted_iota(jnp.int32, (CHUNK, CHUNK), 0) + c * CHUNK
            hit = ((token <= window) & (token > window - CHUNK)) | (window == 15 * CHUNK + mid)
            matrix = jnp.concatenate((sums[0], sums[1], sums[2], jnp.where(hit, 1.0, 0.0).astype(BF16)), axis=1)
            result = dot(pieces, matrix)
            results.append(result[:heads] + result[heads : 2 * heads] + result[2 * heads :])
        for c, result in zip(batch, results):
            centred = result[:, :CHUNK]
            values = []
            for value in (
                jnp.exp(-centred) * stepbuf[:, rows_of(c)],
                jnp.exp(centred),
                jnp.exp(before + result[:, CHUNK : 2 * CHUNK]),
            ):
                high = value.astype(BF16).astype(F32)
                values += [high, value - high]
            factors[c] = jnp.concatenate(values, axis=0).T.astype(BF16)
            before = before + result[:, 2 * CHUNK : 3 * CHUNK]
            windows = windows + result[:, 3 * CHUNK :]
        return before, windows

    none = jnp.zeros((heads, CHUNK), F32)
    _, windows = lax.fori_loop(0, chunks // BATCH, decays, (none, none))
    head_rows = jnp.exp(windows).T[:16]
    lam_row = jnp.concatenate(split3(head_rows[15:16]) + (jnp.zeros((1, LANES - 3 * heads), BF16),), axis=1)
    lam_tile = jnp.broadcast_to(lam_row.astype(F32), (part_rows, LANES)).astype(BF16)

    def put_lam(d, _):
        parts[d, TILES] = lam_tile
        return 0

    lax.fori_loop(0, ctx_size, put_lam, 0)
    row_at = lax.broadcasted_iota(jnp.int32, (16, heads), 0)
    head_rows = jnp.where(row_at == 14, skip_ref[...], head_rows)
    head_rows = dot(jnp.concatenate(split3(head_rows), axis=1), spread[...])
    for lane in range(groups * TILES):
        rows_ref[lane] = head_rows[:, lane * LANES : (lane + 1) * LANES]

    pl.semaphore_wait(barrier, ctx_size + tp_size - 2)

    right = lax.rem(me + 1, ctx_size)

    def halo_copy(src, dst, at):
        return pltpu.make_async_remote_copy(
            src_ref=src, dst_ref=dst, send_sem=halo_send.at[at], recv_sem=halo_recv.at[at],
            device_id=(right, tp), device_id_type=MESH,
        )

    halos = [
        halo_copy(bcbuf.at[:, pl.ds(length, HALO)], bcbuf.at[:, pl.ds(0, HALO)], 0),
        halo_copy(xbuf.at[:, pl.ds(length, HALO)], xbuf.at[:, pl.ds(0, HALO)], 1),
    ]

    def part_copy(src, dst, to):
        return pltpu.make_async_remote_copy(
            src_ref=src, dst_ref=dst, send_sem=part_send.at[0], recv_sem=part_recv.at[0],
            device_id=(to, tp), device_id_type=MESH,
        )

    def start_copy(src, dst, to):
        return pltpu.make_async_remote_copy(
            src_ref=src, dst_ref=dst, send_sem=start_send.at[0], recv_sem=start_recv.at[0],
            device_id=(to, tp), device_id_type=MESH,
        )

    def ssq_copy(dst, src):
        return pltpu.make_async_remote_copy(
            src_ref=ssq, dst_ref=ssq_recv.at[src], send_sem=ssq_send.at[dst],
            recv_sem=ssq_recv_sem.at[src], device_id=(me, dst), device_id_type=MESH,
        )

    def each_tp(fn):
        def step(k, _):
            fn(lax.rem(tp + k, tp_size))
            return 0

        lax.fori_loop(1, tp_size, step, 0)

    others = pl.ds(0, ctx_size - 1)
    all_parts = part_copy(parts.at[others], recv.at[others], right)
    all_starts = start_copy(send.at[others], send.at[others], right)

    for load in bc_loads:
        load.wait()
    halos[0].start()

    bc_taps = [0.5 * convbc_ref[k : k + 1, :] for k in range(4)]

    def project(b):
        batch = [b * BATCH + k for k in range(BATCH)]
        blocks, moved = [], []
        for c in batch:
            rows = pl.ds(pl.multiple_of(c * CHUNK, CHUNK), CHUNK + HALO)
            blocks.append(jnp.concatenate((bcbuf[0, rows], bcbuf[1, rows]), axis=1))
        for block in blocks:
            moved.append(dot(shift_one[...], block))
        turned, c_rows = [], []
        for c, block, move in zip(batch, blocks, moved):
            half = bc_taps[3] * block[HALO:].astype(F32)
            for by in range(1, 4):
                half = half + bc_taps[3 - by] * move[(by - 1) * CHUNK : by * CHUNK]
            both = silu_of_half(half).astype(BF16)
            c_rows.append(both[:, n_state:])
            turned.append(both[:, :n_state].T)
            bt[c] = turned[-1]
            c_ref[c] = c_rows[-1]
        causal = lax.broadcasted_iota(jnp.int32, (CHUNK, CHUNK), 0) >= lax.broadcasted_iota(
            jnp.int32, (CHUNK, CHUNK), 1
        )
        scores = [dot(c_row, b_turned) for c_row, b_turned in zip(c_rows, turned)]
        for c, score in zip(batch, scores):
            scores_ref[c] = jnp.where(causal, score, 0.0).astype(BF16)

    def project_step(b, _):
        @pl.when(b == 0)
        def _():
            for k in range(groups * TILES):
                x_load(k).wait()
            halos[1].start()
            for halo, ref in zip(halos, (bcbuf, xbuf)):
                halo.wait_recv()
                for k in range(ref.shape[0]):
                    ref[k, 0:HALO] = jnp.where(me > 0, ref[k, 0:HALO].astype(F32), 0.0).astype(BF16)

        project(b)
        return 0

    last = chunks // BATCH - 1
    lax.fori_loop(0, chunks // BATCH, lambda k, v: project_step(last - k, v), 0)

    def carry_through():
        all_parts.wait_recv()
        col = pl.multiple_of(mine * GROUP, GROUP)
        decay = recv[:, TILES].reshape(ctx_size * part_rows, LANES)[:, : 3 * heads]
        decay = dot(decay, spread[:, pl.ds(col, GROUP)])
        lam_wide[...] = decay.reshape(ctx_size, part_rows, GROUP)

        def step(d, running):
            for k in range(TILES):
                send[d, k] = running[:, k * LANES : (k + 1) * LANES].astype(BF16)
            arrived = jnp.concatenate([recv[d, k] for k in range(TILES)], axis=1)
            return lam_wide[d] * running + arrived.astype(F32)

        lax.fori_loop(0, ctx_size, step, jnp.zeros((part_rows, GROUP), F32), unroll=4)
        here = start_state.at[pl.ds(mine * TILES, TILES), pl.ds(my_row, part_rows)]
        start_state[pl.ds(mine * TILES, TILES), pl.ds(my_row, part_rows)] = send[me]

        def send_start(k, _):
            to = lax.rem(me + k, ctx_size)
            start_copy(send.at[to], here, to).start()
            return 0

        lax.fori_loop(1, ctx_size, send_start, 0)

    batches = chunks // BATCH

    def tap_sums(u):
        g, b = lax.div(u, batches), lax.rem(u, batches)
        col = pl.ds(pl.multiple_of(g * GROUP, GROUP), GROUP)
        taps = [(0.5 * convx_ref[k : k + 1, col]).astype(BF16) for k in range(4)]
        shifts = jnp.concatenate([shift_all[by] for by in range(4)] + [shift_rim[...]], axis=1)

        def one(k):
            at = pl.multiple_of((b * BATCH + k) * CHUNK, CHUNK)
            block = wide(xbuf, g, pl.ds(at, CHUNK + HALO))
            terms = [block * taps[3 - by] for by in range(1, 4)]
            stacked = jnp.concatenate(
                [block[HALO:] * taps[3]] + [term[HALO:] for term in terms] + [term[:HALO] for term in terms], axis=0
            )
            return dot(shifts, stacked)

        return one

    def forward(u, _):
        g, b = lax.div(u, batches), lax.rem(u, batches)
        batch = [b * BATCH + k for k in range(BATCH)]
        factor = factors[pl.ds(b * BATCH, BATCH)].reshape(BATCH * CHUNK, 6 * heads)
        scales = dot(factor, wide(factor_map.at[0], g, slice(None)))
        next_sums = tap_sums(lax.rem(u + 1, groups * batches))
        scaled = []
        for k, c in enumerate(batch):
            value = silu_of_half(ahead[k])
            ahead[k] = next_sums(k)
            put(xconv, g, (rows_of(c),), value.astype(BF16))
            scaled.append((value * scales[k * CHUNK : (k + 1) * CHUNK]).astype(BF16))
            put(xs, g, (c, slice(0, CHUNK)), scaled[-1])
        added = [dot(bt[c], value) for c, value in zip(batch, scaled)]
        held = jnp.where(b == 0, 0.0, state[...])
        for c, more in zip(batch, added):
            put(xs, g, (c, slice(CHUNK, CHUNK + n_state)), held.astype(BF16))
            held = wide(rows_ref, g, pl.ds(c + 1, 1)) * (held + more)
        state[...] = held

        @pl.when(b == batches - 1)
        def _():
            for r in range(per_group):
                for k in range(TILES):
                    parts[r * groups + g, k] = state[
                        r * part_rows : (r + 1) * part_rows, k * LANES : (k + 1) * LANES
                    ].astype(BF16)

            @pl.when(mine == g)
            def _():
                recv[me] = parts[me]

            def send_part(k, _):
                to = lax.rem(me // groups + k, per_group) * groups + g

                @pl.when(to != me)
                def _():
                    part_copy(parts.at[to], recv.at[me], to).start()

                return 0

            lax.fori_loop(0, per_group, send_part, 0)
            pl.when(mine == g - 1)(carry_through)

        return 0

    first_sums = tap_sums(jnp.int32(0))
    for k in range(BATCH):
        ahead[k] = first_sums(k)
    lax.fori_loop(0, groups * batches, forward, 0)

    for k in range(groups * TILES):
        z_load(k).wait()

    def local(b, _):
        batch = [b * PAIR + k for k in range(PAIR)]
        factor = factors[pl.ds(b * PAIR, PAIR)].reshape(PAIR * CHUNK, 6 * heads)
        for g in range(groups):
            inner = [
                dot(
                    jnp.concatenate((scores_ref[c], c_ref[c]), axis=1),
                    wide(xs, g, c),
                )
                for c in batch
            ]
            scales = dot(factor, wide(factor_map.at[1], g, slice(None)))
            reaches = dot(factor, wide(factor_map.at[2], g, slice(None)))
            skip = wide(rows_ref, g, slice(14, 15))
            for k, c in enumerate(batch):
                part = slice(k * CHUNK, (k + 1) * CHUNK)
                gate = silu_of_half((wide(zbuf, g, rows_of(c)) * 0.5).astype(F32))
                skipped = skip * wide(xconv, g, rows_of(c)).astype(F32)
                put(local_ref, g, (rows_of(c),), (inner[k] * scales[part] + skipped) * gate)
                put(gate_ref, g, (rows_of(c),), (reaches[part] * gate).astype(BF16))
        return 0

    half_way = chunks // PAIR // 2
    lax.fori_loop(0, half_way, local, 0)
    pl.when(mine == groups - 1)(carry_through)
    lax.fori_loop(half_way, chunks // PAIR, local, 0)

    all_starts.wait_recv()
    ssq[...] = jnp.zeros_like(ssq)

    def finish(b, _):
        batch = [b * PAIR + k for k in range(PAIR)]
        c_rows = c_ref[pl.ds(b * PAIR, PAIR)].reshape(PAIR * CHUNK, n_state)
        total = [jnp.zeros((CHUNK, LANES), F32) for _ in batch]
        for g in range(groups):
            carried = dot(c_rows, wide(start_state, g, slice(None)))
            for k, c in enumerate(batch):
                gated = wide(local_ref, g, rows_of(c)) + wide(gate_ref, g, rows_of(c)).astype(F32) * carried[
                    k * CHUNK : (k + 1) * CHUNK
                ]
                put(local_ref, g, (rows_of(c),), gated)
                both = gated * gated
                for lane in range(0, GROUP, LANES):
                    total[k] = total[k] + both[:, lane : lane + LANES]
        for k, c in enumerate(batch):
            squares[c] = total[k]
        return 0

    lax.fori_loop(0, chunks // PAIR, finish, 0)

    def turn(b, _):
        for c in [b * BATCH + k for k in range(BATCH)]:
            ssq[pl.ds(c, 1), :] = jnp.sum(squares[c].T, axis=0, keepdims=True)
        return 0

    lax.fori_loop(0, chunks // BATCH, turn, 0)
    ssq_recv[tp] = ssq[...]
    each_tp(lambda d: ssq_copy(d, tp).start())

    for halo in halos:
        halo.wait_send()
    all_parts.wait_send()
    all_starts.wait_send()
    each_tp(lambda s: ssq_copy(s, s).wait_recv())
    mean = jnp.sum(ssq_recv[...], axis=0) * (1.0 / (channels * tp_size))
    inverse[...] = lax.rsqrt(mean + 1e-5)
    each_tp(lambda d: ssq_copy(d, d).wait_send())

    def out_copy(b, lane):
        rows = pl.ds(pl.multiple_of(b * BATCH * CHUNK, CHUNK), BATCH * CHUNK)
        return pltpu.make_async_copy(
            zbuf.at[lane, rows], out_hbm.at[rows, pl.ds(lane * LANES, LANES)], out_sem.at[b, lane]
        )

    def norm(b, _):
        columns = [
            jnp.broadcast_to(inverse[pl.ds(b * BATCH + k, 1), :], (CHUNK, CHUNK)).T for k in range(BATCH)
        ]
        for lane in range(groups * TILES):
            gain = gain_ref[:, lane * LANES : (lane + 1) * LANES]
            for k in range(BATCH):
                at = rows_of(b * BATCH + k)
                zbuf[lane, at] = (local_ref[lane, at] * columns[k] * gain).astype(BF16)
        for lane in range(groups * TILES):
            out_copy(b, lane).start()
        return 0

    lax.fori_loop(0, batches, norm, 0)

    def norm_done(b, _):
        for lane in range(groups * TILES):
            out_copy(b, lane).wait()
        return 0

    lax.fori_loop(0, batches, norm_done, 0)


def per_device(
    x_raw, bc_raw, z_gate, conv_x, conv_bc, step_size, log_decay, skip_scale, norm_gain, *, ctx_size, tp_size
):
    length, channels = x_raw.shape
    heads = step_size.shape[1]
    head_dim = channels // heads
    n_state = bc_raw.shape[1] // 2
    chunks = length // CHUNK
    groups = channels // GROUP
    lanes = channels // LANES
    part_rows = n_state * groups // ctx_size
    in_hbm = pl.BlockSpec(memory_space=pltpu.HBM)
    vmem = pltpu.VMEM
    dma = pltpu.SemaphoreType.DMA
    return pl.pallas_call(
        functools.partial(mixer, ctx_size, tp_size, head_dim),
        out_shape=jax.ShapeDtypeStruct((length, channels), BF16),
        in_specs=[in_hbm] * 9,
        out_specs=in_hbm,
        scratch_shapes=[
            vmem((lanes, length + HALO, LANES), BF16),
            vmem((2, length + HALO, n_state), BF16),
            vmem((lanes, length, LANES), BF16),
            vmem((heads, length), F32),
            vmem((heads, length), F32),
            vmem((4, channels), F32),
            vmem((4, 2 * n_state), F32),
            vmem((1, heads), F32),
            vmem((1, channels), F32),
            vmem((3 * heads, channels), BF16),
            vmem((3, lanes, 6 * heads, LANES), BF16),
            vmem((3 * CHUNK, CHUNK + HALO), BF16),
            vmem((4, CHUNK, CHUNK), BF16),
            vmem((CHUNK, 3 * HALO), BF16),
            vmem((3, CHUNK, CHUNK), BF16),
            vmem((chunks, CHUNK, 6 * heads), BF16),
            vmem((lanes, 16, LANES), F32),
            vmem((chunks, CHUNK, CHUNK), BF16),
            vmem((chunks, CHUNK, n_state), BF16),
            vmem((chunks, n_state, CHUNK), BF16),
            vmem((lanes, length, LANES), BF16),
            vmem((lanes, chunks, CHUNK + n_state, LANES), BF16),
            vmem((n_state, GROUP), F32),
            vmem((ctx_size, TILES + 1, part_rows, LANES), BF16),
            vmem((ctx_size, TILES + 1, part_rows, LANES), BF16),
            vmem((ctx_size, part_rows, GROUP), F32),
            vmem((ctx_size, TILES, part_rows, LANES), BF16),
            vmem((lanes, n_state, LANES), BF16),
            vmem((BATCH, CHUNK, GROUP), F32),
            vmem((lanes, length, LANES), F32),
            vmem((lanes, length, LANES), BF16),
            vmem((chunks, CHUNK, LANES), F32),
            vmem((16, 128), F32),
            vmem((tp_size, 16, 128), F32),
            vmem((16, 128), F32),
            dma((8 + 2 * lanes,)),
            dma((2,)),
            dma((2,)),
            dma((1,)),
            dma((1,)),
            dma((1,)),
            dma((1,)),
            dma((tp_size,)),
            dma((tp_size,)),
            dma((chunks // BATCH, lanes)),
        ],
        compiler_params=pltpu.CompilerParams(
            collective_id=0, has_side_effects=True, vmem_limit_bytes=56 * 1024 * 1024
        ),
        name="mixer",
    )(
        x_raw, bc_raw, z_gate, conv_x, conv_bc, step_size.T, log_decay.T,
        skip_scale.reshape(1, heads), norm_gain.reshape(1, channels),
    )


def solution(mesh):
    sizes = dict(mesh.shape)
    return jax.shard_map(
        functools.partial(per_device, ctx_size=sizes["ctx"], tp_size=sizes["tp"]),
        mesh=mesh,
        in_specs=(
            P("ctx", "tp"),
            P("ctx", None),
            P("ctx", "tp"),
            P(None, "tp"),
            P(),
            P("ctx", "tp"),
            P("ctx", "tp"),
            P("tp"),
            P("tp"),
        ),
        out_specs=P("ctx", "tp"),
        check_vma=False,
    )
```

```python
import functools

import jax
import jax.numpy as jnp
from jax import lax
from jax.experimental import pallas as pl
from jax.experimental.pallas import tpu as pltpu
from jax.sharding import PartitionSpec as P

F32 = jnp.float32
BF16 = jnp.bfloat16
MESH = pl.DeviceIdType.MESH
CHUNK = 128
LANES = 128
GROUP = 256
TILES = GROUP // LANES
HALO = 16
BATCH = 4
PAIR = 2


def split3(value):
    high = value.astype(BF16)
    rest = value - high.astype(F32)
    mid = rest.astype(BF16)
    return high, mid, (rest - mid.astype(F32)).astype(BF16)


def silu_of_half(half):
    return half * jnp.tanh(half) + half


def dot(left, right):
    return jnp.dot(left, right, preferred_element_type=F32)


def each_other(size, fn):
    count = size - 1
    unroll = next(n for n in (6, 5, 4, 3, 2, 1) if (count - 1) % n == 0)

    def step(k, _):
        fn(k)
        return 0

    if count > 1:
        lax.fori_loop(1, count, step, 0, unroll=unroll)
    fn(count)


def mixer(
    ctx_size, tp_size, head_dim,
    x_hbm, bc_hbm, z_hbm, convx_hbm, convbc_hbm, step_hbm, log_hbm, skip_hbm, gain_hbm,
    out_ref,
    xbuf, bcbuf, zbuf, x_rim, bc_rim, stepbuf, logbuf, convx_ref, convbc_ref, skip_ref, gain_ref,
    spread, factor_map, shift_one, shift_all, shift_rim, sums, factors, rows_ref,
    scores_ref, c_ref, bt, xconv, xs, state, parts, recv, lam_wide, send, start_state,
    ahead, local_ref, gate_ref, squares, ssq, ssq_recv,
    load_sem, halo_send, halo_recv, part_send, part_recv, start_send, start_recv, ssq_send, ssq_recv_sem,
):
    length, channels = x_hbm.shape
    heads = step_hbm.shape[0]
    chunks = length // CHUNK
    groups = channels // GROUP
    n_state = bt.shape[1]
    part_rows = parts.shape[2]
    per_group = ctx_size // groups
    mid = CHUNK // 2 - 1
    me = lax.axis_index("ctx")
    tp = lax.axis_index("tp")
    mine = lax.rem(me, groups)
    my_row = pl.multiple_of((me // groups) * part_rows, part_rows)

    def wide(ref, g, *at):
        return jnp.concatenate([ref[(g * TILES + k, *at)] for k in range(TILES)], axis=-1)

    def put(ref, g, at, value):
        for k in range(TILES):
            ref[(g * TILES + k, *at)] = value[:, k * LANES : (k + 1) * LANES]

    def rows_of(c):
        return pl.ds(pl.multiple_of(c * CHUNK, CHUNK), CHUNK)

    small_loads = [
        pltpu.make_async_copy(src, dst, load_sem.at[k])
        for k, (src, dst) in enumerate(
            (
                (log_hbm, logbuf),
                (step_hbm, stepbuf),
                (skip_hbm, skip_ref),
                (convbc_hbm, convbc_ref),
                (convx_hbm, convx_ref),
                (gain_hbm, gain_ref),
            )
        )
    ]
    bc_loads = [
        pltpu.make_async_copy(
            bc_hbm.at[:, pl.ds(k * LANES, LANES)], bcbuf.at[k, pl.ds(HALO, length)], load_sem.at[6 + k]
        )
        for k in range(2)
    ]

    def x_load(k):
        col = pl.ds(pl.multiple_of(k * LANES, LANES), LANES)
        return pltpu.make_async_copy(x_hbm.at[:, col], xbuf.at[k, pl.ds(HALO, length)], load_sem.at[8 + k])

    def z_load(k):
        col = pl.ds(pl.multiple_of(k * LANES, LANES), LANES)
        return pltpu.make_async_copy(
            z_hbm.at[:, col], zbuf.at[k], load_sem.at[8 + groups * TILES + k]
        )

    for load in small_loads + bc_loads:
        load.start()
    for k in range(groups * TILES):
        x_load(k).start()
    for k in range(groups * TILES):
        z_load(k).start()

    barrier = pltpu.get_barrier_semaphore()

    def greet_ctx(k):
        pl.semaphore_signal(barrier, inc=1, device_id=(lax.rem(me + k, ctx_size), tp), device_id_type=MESH)

    def greet_tp(k):
        pl.semaphore_signal(barrier, inc=1, device_id=(me, lax.rem(tp + k, tp_size)), device_id_type=MESH)

    each_other(ctx_size, greet_ctx)
    each_other(tp_size, greet_tp)

    pl.semaphore_wait(barrier, ctx_size + tp_size - 2)

    right = lax.rem(me + 1, ctx_size)

    def halo_copy(src, dst, at):
        return pltpu.make_async_remote_copy(
            src_ref=src.at[pl.ds(length - HALO, HALO)], dst_ref=dst, send_sem=halo_send.at[at],
            recv_sem=halo_recv.at[at], device_id=(right, tp), device_id_type=MESH,
        )

    halos = [halo_copy(bc_hbm, bc_rim, 0), halo_copy(x_hbm, x_rim, 1)]
    for halo in halos:
        halo.start()

    s_at = lax.broadcasted_iota(jnp.int32, (CHUNK, CHUNK), 0)
    t_at = lax.broadcasted_iota(jnp.int32, (CHUNK, CHUNK), 1)
    upto = jnp.where(s_at <= t_at, 1.0, 0.0)
    sums[0] = (upto - jnp.where(s_at <= mid, 1.0, 0.0)).astype(BF16)
    sums[1] = upto.astype(BF16)
    sums[2] = jnp.ones((CHUNK, CHUNK), BF16)

    head_at = lax.broadcasted_iota(jnp.int32, (heads, channels), 0)
    channel_at = lax.broadcasted_iota(jnp.int32, (heads, channels), 1)
    first = head_at * head_dim
    one_map = jnp.where((channel_at >= first) & (channel_at < first + head_dim), 1.0, 0.0).astype(BF16)
    factor_map[...] = jnp.zeros_like(factor_map)
    for k in range(3):
        spread[k * heads : (k + 1) * heads, :] = one_map
        for term in range(2):
            row = (2 * k + term) * heads
            for lane in range(groups * TILES):
                factor_map[k, lane, row : row + heads, :] = one_map[:, lane * LANES : (lane + 1) * LANES]

    def shift(by, width, before):
        to = lax.broadcasted_iota(jnp.int32, (CHUNK, width), 0)
        at = lax.broadcasted_iota(jnp.int32, (CHUNK, width), 1)
        return jnp.where(to + (before - by) == at, 1.0, 0.0).astype(BF16)

    for by in range(4):
        shift_all[by] = shift(by, CHUNK, 0)
        if by > 0:
            shift_one[(by - 1) * CHUNK : by * CHUNK, :] = shift(by, CHUNK + HALO, HALO)
    halo_to = lax.broadcasted_iota(jnp.int32, (CHUNK, 3 * HALO), 0)
    halo_at = lax.broadcasted_iota(jnp.int32, (CHUNK, 3 * HALO), 1)
    halo_hit = halo_to < 0
    for by in range(1, 4):
        inside = (halo_at >= (by - 1) * HALO) & (halo_at < by * HALO)
        halo_hit = halo_hit | ((halo_to + (by * HALO - by) == halo_at) & inside)
    shift_rim[...] = jnp.where(halo_hit, 1.0, 0.0).astype(BF16)

    for load in small_loads:
        load.wait()

    def decays(b, carry):
        before, windows = carry
        batch = [b * BATCH + k for k in range(BATCH)]
        window = lax.broadcasted_iota(jnp.int32, (CHUNK, CHUNK), 1) * CHUNK + mid
        results = []
        for c in batch:
            pieces = jnp.concatenate(split3(logbuf[:, rows_of(c)]), axis=0)
            token = lax.broadcasted_iota(jnp.int32, (CHUNK, CHUNK), 0) + c * CHUNK
            hit = ((token <= window) & (token > window - CHUNK)) | (window == 15 * CHUNK + mid)
            matrix = jnp.concatenate((sums[0], sums[1], sums[2], jnp.where(hit, 1.0, 0.0).astype(BF16)), axis=1)
            result = dot(pieces, matrix)
            results.append(result[:heads] + result[heads : 2 * heads] + result[2 * heads :])
        for c, result in zip(batch, results):
            centred = result[:, :CHUNK]
            values = []
            for value in (
                jnp.exp(-centred) * stepbuf[:, rows_of(c)],
                jnp.exp(centred),
                jnp.exp(before + result[:, CHUNK : 2 * CHUNK]),
            ):
                high = value.astype(BF16).astype(F32)
                values += [high, value - high]
            factors[c] = jnp.concatenate(values, axis=0).T.astype(BF16)
            before = before + result[:, 2 * CHUNK : 3 * CHUNK]
            windows = windows + result[:, 3 * CHUNK :]
        return before, windows

    none = jnp.zeros((heads, CHUNK), F32)
    _, windows = lax.fori_loop(0, chunks // BATCH, decays, (none, none))
    head_rows = jnp.exp(windows).T[:16]
    lam_row = jnp.concatenate(split3(head_rows[15:16]) + (jnp.zeros((1, LANES - 3 * heads), BF16),), axis=1)
    lam_tile = jnp.broadcast_to(lam_row.astype(F32), (part_rows, LANES)).astype(BF16)

    def put_lam(d, _):
        parts[d, TILES] = lam_tile
        return 0

    lax.fori_loop(0, ctx_size, put_lam, 0, unroll=4)
    row_at = lax.broadcasted_iota(jnp.int32, (16, heads), 0)
    head_rows = jnp.where(row_at == 14, skip_ref[...], head_rows)
    head_rows = dot(jnp.concatenate(split3(head_rows), axis=1), spread[...])
    for lane in range(groups * TILES):
        rows_ref[lane] = head_rows[:, lane * LANES : (lane + 1) * LANES]

    def part_copy(src, dst, to):
        return pltpu.make_async_remote_copy(
            src_ref=src, dst_ref=dst, send_sem=part_send.at[0], recv_sem=part_recv.at[0],
            device_id=(to, tp), device_id_type=MESH,
        )

    def start_copy(src, dst, to):
        return pltpu.make_async_remote_copy(
            src_ref=src, dst_ref=dst, send_sem=start_send.at[0], recv_sem=start_recv.at[0],
            device_id=(to, tp), device_id_type=MESH,
        )

    def ssq_copy(p, to):
        return pltpu.make_async_remote_copy(
            src_ref=ssq.at[p], dst_ref=ssq_recv.at[p, tp], send_sem=ssq_send.at[p],
            recv_sem=ssq_recv_sem.at[p], device_id=(me, to), device_id_type=MESH,
        )

    def all_ssq(p):
        others = ssq_recv.at[p, pl.ds(0, tp_size - 1)]
        return pltpu.make_async_remote_copy(
            src_ref=others, dst_ref=others, send_sem=ssq_send.at[p], recv_sem=ssq_recv_sem.at[p],
            device_id=(me, tp), device_id_type=MESH,
        )

    others = pl.ds(0, ctx_size - 1)
    all_parts = part_copy(parts.at[others], recv.at[others], right)
    all_starts = start_copy(send.at[others], send.at[others], right)

    for load in bc_loads:
        load.wait()

    bc_taps = [0.5 * convbc_ref[k : k + 1, :] for k in range(4)]

    def project(b):
        batch = [b * BATCH + k for k in range(BATCH)]
        blocks, moved = [], []
        for c in batch:
            rows = pl.ds(pl.multiple_of(c * CHUNK, CHUNK), CHUNK + HALO)
            blocks.append(jnp.concatenate((bcbuf[0, rows], bcbuf[1, rows]), axis=1))
        for block in blocks:
            moved.append(dot(shift_one[...], block))
        turned, c_rows = [], []
        for c, block, move in zip(batch, blocks, moved):
            half = bc_taps[3] * block[HALO:].astype(F32)
            for by in range(1, 4):
                half = half + bc_taps[3 - by] * move[(by - 1) * CHUNK : by * CHUNK]
            both = silu_of_half(half).astype(BF16)
            c_rows.append(both[:, n_state:])
            turned.append(both[:, :n_state].T)
            bt[c] = turned[-1]
            c_ref[c] = c_rows[-1]
        causal = lax.broadcasted_iota(jnp.int32, (CHUNK, CHUNK), 0) >= lax.broadcasted_iota(
            jnp.int32, (CHUNK, CHUNK), 1
        )
        scores = [dot(c_row, b_turned) for c_row, b_turned in zip(c_rows, turned)]
        for c, score in zip(batch, scores):
            scores_ref[c] = jnp.where(causal, score, 0.0).astype(BF16)

    def project_step(b, _):
        @pl.when(b == 0)
        def _():
            for k in range(groups * TILES):
                x_load(k).wait()
            for halo, rim, ref in zip(halos, (bc_rim, x_rim), (bcbuf, xbuf)):
                halo.wait_recv()
                for k in range(ref.shape[0]):
                    before = rim[:, k * LANES : (k + 1) * LANES].astype(F32)
                    ref[k, 0:HALO] = jnp.where(me > 0, before, 0.0).astype(BF16)

        project(b)
        return 0

    last = chunks // BATCH - 1
    lax.fori_loop(0, chunks // BATCH, lambda k, v: project_step(last - k, v), 0)

    def carry_through():
        all_parts.wait_recv()
        col = pl.multiple_of(mine * GROUP, GROUP)
        decay = recv[:, TILES].reshape(ctx_size * part_rows, LANES)[:, : 3 * heads]
        decay = dot(decay, spread[:, pl.ds(col, GROUP)])
        lam_wide[...] = decay.reshape(ctx_size, part_rows, GROUP)

        def step(d, running):
            for k in range(TILES):
                send[d, k] = running[:, k * LANES : (k + 1) * LANES].astype(BF16)
            arrived = jnp.concatenate([recv[d, k] for k in range(TILES)], axis=1)
            return lam_wide[d] * running + arrived.astype(F32)

        lax.fori_loop(0, ctx_size, step, jnp.zeros((part_rows, GROUP), F32), unroll=4)
        here = start_state.at[pl.ds(mine * TILES, TILES), pl.ds(my_row, part_rows)]
        start_state[pl.ds(mine * TILES, TILES), pl.ds(my_row, part_rows)] = send[me]

        def send_start(k):
            to = lax.rem(me + k, ctx_size)
            start_copy(send.at[to], here, to).start()

        each_other(ctx_size, send_start)

    batches = chunks // BATCH

    def tap_sums(u):
        g, b = lax.div(u, batches), lax.rem(u, batches)
        col = pl.ds(pl.multiple_of(g * GROUP, GROUP), GROUP)
        taps = [(0.5 * convx_ref[k : k + 1, col]).astype(BF16) for k in range(4)]
        shifts = jnp.concatenate([shift_all[by] for by in range(4)] + [shift_rim[...]], axis=1)

        def one(k):
            at = pl.multiple_of((b * BATCH + k) * CHUNK, CHUNK)
            block = wide(xbuf, g, pl.ds(at, CHUNK + HALO))
            terms = [block * taps[3 - by] for by in range(1, 4)]
            stacked = jnp.concatenate(
                [block[HALO:] * taps[3]] + [term[HALO:] for term in terms] + [term[:HALO] for term in terms], axis=0
            )
            return dot(shifts, stacked)

        return one

    def advance(u):
        g, b = lax.div(u, batches), lax.rem(u, batches)
        batch = [b * BATCH + k for k in range(BATCH)]
        added = [dot(bt[c], wide(xs, g, c, slice(0, CHUNK))) for c in batch]

        def follow():
            held = jnp.where(b == 0, 0.0, state[...])
            for c, more in zip(batch, added):
                put(xs, g, (c, slice(CHUNK, CHUNK + n_state)), held.astype(BF16))
                held = wide(rows_ref, g, pl.ds(c + 1, 1)) * (held + more)
            state[...] = held

        return follow

    def leave(g):
        for r in range(per_group):
            for k in range(TILES):
                parts[r * groups + g, k] = state[
                    r * part_rows : (r + 1) * part_rows, k * LANES : (k + 1) * LANES
                ].astype(BF16)

        def send_part(k):
            to = lax.rem(me // groups + k, per_group) * groups + g
            part_copy(parts.at[to], recv.at[me], to).start()

        @pl.when(mine == g)
        def _():
            recv[me] = parts[me]

        @pl.when(mine != g)
        def _():
            send_part(0)

        if per_group > 1:
            each_other(per_group, send_part)

    def forward(u, _):
        g, b = lax.div(u, batches), lax.rem(u, batches)
        batch = [b * BATCH + k for k in range(BATCH)]
        last_u = lax.max(u - 1, 0)
        factor = factors[pl.ds(b * BATCH, BATCH)].reshape(BATCH * CHUNK, 6 * heads)
        scales = dot(factor, wide(factor_map.at[0], g, slice(None)))
        follow = advance(last_u)
        next_sums = tap_sums(lax.rem(u + 1, groups * batches))
        for k, c in enumerate(batch):
            value = silu_of_half(ahead[k])
            ahead[k] = next_sums(k)
            put(xconv, g, (rows_of(c),), value.astype(BF16))
            put(xs, g, (c, slice(0, CHUNK)), (value * scales[k * CHUNK : (k + 1) * CHUNK]).astype(BF16))
        follow()

        @pl.when((b == 0) & (u > 0))
        def _():
            leave(g - 1)
            pl.when(mine == g - 3)(carry_through)

        return 0

    first_sums = tap_sums(jnp.int32(0))
    for k in range(BATCH):
        ahead[k] = first_sums(k)
    lax.fori_loop(0, groups * batches, forward, 0)
    advance(groups * batches - 1)()
    leave(groups - 1)
    pl.when(mine == groups - 3)(carry_through)

    for k in range(groups * TILES):
        z_load(k).wait()

    def local(b, _):
        batch = [b * PAIR + k for k in range(PAIR)]
        factor = factors[pl.ds(b * PAIR, PAIR)].reshape(PAIR * CHUNK, 6 * heads)
        for g in range(groups):
            inner = [
                dot(
                    jnp.concatenate((scores_ref[c], c_ref[c]), axis=1),
                    wide(xs, g, c),
                )
                for c in batch
            ]
            scales = dot(factor, wide(factor_map.at[1], g, slice(None)))
            reaches = dot(factor, wide(factor_map.at[2], g, slice(None)))
            skip = wide(rows_ref, g, slice(14, 15))
            for k, c in enumerate(batch):
                part = slice(k * CHUNK, (k + 1) * CHUNK)
                gate = silu_of_half((wide(zbuf, g, rows_of(c)) * 0.5).astype(F32))
                skipped = skip * wide(xconv, g, rows_of(c)).astype(F32)
                put(local_ref, g, (rows_of(c),), (inner[k] * scales[part] + skipped) * gate)
                put(gate_ref, g, (rows_of(c),), (reaches[part] * gate).astype(BF16))
        return 0

    def local_step(b, _):
        pl.when((b >= 1) & (mine == b + (groups - 3)))(carry_through)
        return local(b, 0)

    lax.fori_loop(0, chunks // PAIR, local_step, 0)

    all_starts.wait_recv()
    def finish(b, _):
        batch = [b * PAIR + k for k in range(PAIR)]
        c_rows = c_ref[pl.ds(b * PAIR, PAIR)].reshape(PAIR * CHUNK, n_state)
        total = [jnp.zeros((CHUNK, LANES), F32) for _ in batch]
        for g in range(groups):
            carried = dot(c_rows, wide(start_state, g, slice(None)))
            for k, c in enumerate(batch):
                gated = wide(local_ref, g, rows_of(c)) + wide(gate_ref, g, rows_of(c)).astype(F32) * carried[
                    k * CHUNK : (k + 1) * CHUNK
                ]
                put(local_ref, g, (rows_of(c),), gated)
                both = gated * gated
                for lane in range(0, GROUP, LANES):
                    total[k] = total[k] + both[:, lane : lane + LANES]
        for k, c in enumerate(batch):
            squares[c] = total[k]
        return 0

    def piece(p, _):
        for k in range(BATCH // PAIR):
            finish(p * (BATCH // PAIR) + k, 0)
        for k in range(BATCH):
            ssq[p, k : k + 1, :] = jnp.sum(squares[p * BATCH + k].T, axis=0, keepdims=True)
        ssq[p, BATCH:, :] = jnp.zeros((8 - BATCH, LANES), F32)
        ssq_recv[p, tp] = ssq[p]
        each_other(tp_size, lambda k: ssq_copy(p, lax.rem(tp + k, tp_size)).start())
        return 0

    lax.fori_loop(0, batches, piece, 0)

    for halo in halos:
        halo.wait_send()
    all_parts.wait_send()
    all_starts.wait_send()

    def norm(b, _):
        all_ssq(b).wait_recv()
        mean = jnp.sum(ssq_recv[b], axis=0) * (1.0 / (channels * tp_size))
        inverse = lax.rsqrt(mean + 1e-5)
        columns = [jnp.broadcast_to(inverse[k : k + 1], (CHUNK, CHUNK)).T for k in range(BATCH)]
        for lane in range(groups * TILES):
            here = slice(lane * LANES, (lane + 1) * LANES)
            for k in range(BATCH):
                at = rows_of(b * BATCH + k)
                out_ref[at, here] = (local_ref[lane, at] * columns[k] * gain_ref[:, here]).astype(BF16)
        return 0

    lax.fori_loop(0, batches, norm, 0)
    for b in range(batches):
        all_ssq(b).wait_send()


def per_device(
    x_raw, bc_raw, z_gate, conv_x, conv_bc, step_size, log_decay, skip_scale, norm_gain, *, ctx_size, tp_size
):
    length, channels = x_raw.shape
    heads = step_size.shape[1]
    head_dim = channels // heads
    n_state = bc_raw.shape[1] // 2
    chunks = length // CHUNK
    groups = channels // GROUP
    lanes = channels // LANES
    part_rows = n_state * groups // ctx_size
    in_hbm = pl.BlockSpec(memory_space=pltpu.HBM)
    vmem = pltpu.VMEM
    dma = pltpu.SemaphoreType.DMA
    return pl.pallas_call(
        functools.partial(mixer, ctx_size, tp_size, head_dim),
        out_shape=pltpu.VMEM((length, channels), BF16),
        in_specs=[in_hbm] * 9,
        out_specs=pl.BlockSpec(memory_space=pltpu.VMEM),
        scratch_shapes=[
            vmem((lanes, length + HALO, LANES), BF16),
            vmem((2, length + HALO, n_state), BF16),
            vmem((lanes, length, LANES), BF16),
            vmem((HALO, channels), BF16),
            vmem((HALO, 2 * n_state), BF16),
            vmem((heads, length), F32),
            vmem((heads, length), F32),
            vmem((4, channels), F32),
            vmem((4, 2 * n_state), F32),
            vmem((1, heads), F32),
            vmem((1, channels), F32),
            vmem((3 * heads, channels), BF16),
            vmem((3, lanes, 6 * heads, LANES), BF16),
            vmem((3 * CHUNK, CHUNK + HALO), BF16),
            vmem((4, CHUNK, CHUNK), BF16),
            vmem((CHUNK, 3 * HALO), BF16),
            vmem((3, CHUNK, CHUNK), BF16),
            vmem((chunks, CHUNK, 6 * heads), BF16),
            vmem((lanes, 16, LANES), F32),
            vmem((chunks, CHUNK, CHUNK), BF16),
            vmem((chunks, CHUNK, n_state), BF16),
            vmem((chunks, n_state, CHUNK), BF16),
            vmem((lanes, length, LANES), BF16),
            vmem((lanes, chunks, CHUNK + n_state, LANES), BF16),
            vmem((n_state, GROUP), F32),
            vmem((ctx_size, TILES + 1, part_rows, LANES), BF16),
            vmem((ctx_size, TILES + 1, part_rows, LANES), BF16),
            vmem((ctx_size, part_rows, GROUP), F32),
            vmem((ctx_size, TILES, part_rows, LANES), BF16),
            vmem((lanes, n_state, LANES), BF16),
            vmem((BATCH, CHUNK, GROUP), F32),
            vmem((lanes, length, LANES), F32),
            vmem((lanes, length, LANES), BF16),
            vmem((chunks, CHUNK, LANES), F32),
            vmem((chunks // BATCH, 8, LANES), F32),
            vmem((chunks // BATCH, tp_size, 8, LANES), F32),
            dma((8 + 2 * lanes,)),
            dma((2,)),
            dma((2,)),
            dma((1,)),
            dma((1,)),
            dma((1,)),
            dma((1,)),
            dma((chunks // BATCH,)),
            dma((chunks // BATCH,)),
        ],
        compiler_params=pltpu.CompilerParams(
            collective_id=0, has_side_effects=True, vmem_limit_bytes=56 * 1024 * 1024
        ),
        name="mixer",
    )(
        x_raw, bc_raw, z_gate, conv_x, conv_bc, step_size.T, log_decay.T,
        skip_scale.reshape(1, heads), norm_gain.reshape(1, channels),
    )


def solution(mesh):
    sizes = dict(mesh.shape)
    return jax.shard_map(
        functools.partial(per_device, ctx_size=sizes["ctx"], tp_size=sizes["tp"]),
        mesh=mesh,
        in_specs=(
            P("ctx", "tp"),
            P("ctx", None),
            P("ctx", "tp"),
            P(None, "tp"),
            P(),
            P("ctx", "tp"),
            P("ctx", "tp"),
            P("tp"),
            P("tp"),
        ),
        out_specs=P("ctx", "tp"),
        check_vma=False,
    )
```

```python
import functools

import jax
import jax.numpy as jnp
from jax import lax
from jax.experimental import pallas as pl
from jax.experimental.pallas import tpu as pltpu
from jax.sharding import PartitionSpec as P

F32 = jnp.float32
BF16 = jnp.bfloat16
MESH = pl.DeviceIdType.MESH
CHUNK = 128
LANES = 128
GROUP = 256
TILES = GROUP // LANES
HALO = 16
BATCH = 4
PAIR = 2


def split3(value):
    high = value.astype(BF16)
    rest = value - high.astype(F32)
    mid = rest.astype(BF16)
    return high, mid, (rest - mid.astype(F32)).astype(BF16)


def silu_of_half(half):
    return half * jnp.tanh(half) + half


def dot(left, right):
    return jnp.dot(left, right, preferred_element_type=F32)


def each_other(size, fn):
    count = size - 1
    unroll = next(n for n in (6, 5, 4, 3, 2, 1) if (count - 1) % n == 0)

    def step(k, _):
        fn(k)
        return 0

    if count > 1:
        lax.fori_loop(1, count, step, 0, unroll=unroll)
    fn(count)


def mixer(
    ctx_size, tp_size, head_dim,
    x_hbm, bc_hbm, z_hbm, convx_hbm, convbc_hbm, step_hbm, log_hbm, skip_hbm, gain_hbm,
    out_ref,
    xbuf, bcbuf, zbuf, x_rim, bc_rim, stepbuf, logbuf, convx_ref, convbc_ref, skip_ref, gain_ref,
    spread, factor_map, shift_one, shift_all, shift_rim, sums, factors, rows_ref,
    scores_ref, c_ref, bt, xconv, xs, state, parts, recv, lam_wide, send, start_state,
    ahead, local_ref, gate_ref, squares, ssq, ssq_recv,
    load_sem, halo_send, halo_recv, part_send, part_recv, start_send, start_recv, ssq_send, ssq_recv_sem,
):
    length, channels = x_hbm.shape
    heads = step_hbm.shape[0]
    chunks = length // CHUNK
    groups = channels // GROUP
    n_state = bt.shape[1]
    part_rows = parts.shape[2]
    per_group = ctx_size // groups
    mid = CHUNK // 2 - 1
    me = lax.axis_index("ctx")
    tp = lax.axis_index("tp")
    mine = lax.rem(me // 2 + me // 8, 2) * 2 + lax.rem(me, 2)
    my_row = pl.multiple_of((me // groups) * part_rows, part_rows)

    def carrier(g, r):
        return r * groups + lax.rem(g // 2 + r // 2, 2) * 2 + lax.rem(g, 2)

    def wide(ref, g, *at):
        return jnp.concatenate([ref[(g * TILES + k, *at)] if at else ref[g * TILES + k] for k in range(TILES)], axis=-1)

    def put(ref, g, at, value):
        for k in range(TILES):
            ref[(g * TILES + k, *at)] = value[:, k * LANES : (k + 1) * LANES]

    def rows_of(c):
        return pl.ds(pl.multiple_of(c * CHUNK, CHUNK), CHUNK)

    small_loads = [
        pltpu.make_async_copy(src, dst, load_sem.at[k])
        for k, (src, dst) in enumerate(
            (
                (log_hbm, logbuf),
                (step_hbm, stepbuf),
                (skip_hbm, skip_ref),
                (convbc_hbm, convbc_ref),
                (convx_hbm, convx_ref),
                *[
                    (gain_hbm.at[:, pl.ds(k * LANES, LANES)], gain_ref.at[k])
                    for k in range(groups * TILES)
                ],
            )
        )
    ]
    at_bc = len(small_loads)
    bc_loads = [
        pltpu.make_async_copy(
            bc_hbm.at[:, pl.ds(k * LANES, LANES)], bcbuf.at[k, pl.ds(HALO, length)], load_sem.at[at_bc + k]
        )
        for k in range(2)
    ]

    def x_load(k):
        col = pl.ds(pl.multiple_of(k * LANES, LANES), LANES)
        return pltpu.make_async_copy(x_hbm.at[:, col], xbuf.at[k, pl.ds(HALO, length)], load_sem.at[at_bc + 2 + k])

    def z_load(k):
        col = pl.ds(pl.multiple_of(k * LANES, LANES), LANES)
        return pltpu.make_async_copy(
            z_hbm.at[:, col], zbuf.at[k], load_sem.at[at_bc + 2 + groups * TILES + k]
        )

    for load in small_loads + bc_loads:
        load.start()
    for k in range(groups * TILES):
        x_load(k).start()
    for k in range(groups * TILES):
        z_load(k).start()

    barrier = pltpu.get_barrier_semaphore()

    def greet_ctx(k):
        pl.semaphore_signal(barrier, inc=1, device_id=(lax.rem(me + ctx_size - k, ctx_size), tp), device_id_type=MESH)

    def greet_tp(k):
        pl.semaphore_signal(barrier, inc=1, device_id=(me, lax.rem(tp + k, tp_size)), device_id_type=MESH)

    each_other(ctx_size, greet_ctx)
    each_other(tp_size, greet_tp)

    right = lax.rem(me + 1, ctx_size)

    def halo_copy(src, dst, at):
        return pltpu.make_async_remote_copy(
            src_ref=src.at[pl.ds(length - HALO, HALO)], dst_ref=dst, send_sem=halo_send.at[at],
            recv_sem=halo_recv.at[at], device_id=(right, tp), device_id_type=MESH,
        )

    halos = [halo_copy(bc_hbm, bc_rim, 0), halo_copy(x_hbm, x_rim, 1)]
    s_at = lax.broadcasted_iota(jnp.int32, (CHUNK, CHUNK), 0)
    t_at = lax.broadcasted_iota(jnp.int32, (CHUNK, CHUNK), 1)
    upto = jnp.where(s_at <= t_at, 1.0, 0.0)
    sums[0] = (upto - jnp.where(s_at <= mid, 1.0, 0.0)).astype(BF16)
    sums[1] = upto.astype(BF16)
    sums[2] = jnp.ones((CHUNK, CHUNK), BF16)

    head_at = lax.broadcasted_iota(jnp.int32, (heads, channels), 0)
    channel_at = lax.broadcasted_iota(jnp.int32, (heads, channels), 1)
    first = head_at * head_dim
    one_map = jnp.where((channel_at >= first) & (channel_at < first + head_dim), 1.0, 0.0).astype(BF16)
    factor_map[...] = jnp.zeros_like(factor_map)
    for k in range(3):
        spread[k * heads : (k + 1) * heads, :] = one_map
        for term in range(2):
            row = (2 * k + term) * heads
            for lane in range(groups * TILES):
                factor_map[k, lane, row : row + heads, :] = one_map[:, lane * LANES : (lane + 1) * LANES]

    def shift(by, width, before):
        to = lax.broadcasted_iota(jnp.int32, (CHUNK, width), 0)
        at = lax.broadcasted_iota(jnp.int32, (CHUNK, width), 1)
        return jnp.where(to + (before - by) == at, 1.0, 0.0).astype(BF16)

    for by in range(4):
        shift_all[by] = shift(by, CHUNK, 0)
        if by > 0:
            shift_one[(by - 1) * CHUNK : by * CHUNK, :] = shift(by, CHUNK + HALO, HALO)
    halo_to = lax.broadcasted_iota(jnp.int32, (CHUNK, 3 * HALO), 0)
    halo_at = lax.broadcasted_iota(jnp.int32, (CHUNK, 3 * HALO), 1)
    halo_hit = halo_to < 0
    for by in range(1, 4):
        inside = (halo_at >= (by - 1) * HALO) & (halo_at < by * HALO)
        halo_hit = halo_hit | ((halo_to + (by * HALO - by) == halo_at) & inside)
    shift_rim[...] = jnp.where(halo_hit, 1.0, 0.0).astype(BF16)

    for load in small_loads:
        load.wait()

    def decays(b, carry):
        before, windows = carry
        batch = [b * BATCH + k for k in range(BATCH)]
        window = lax.broadcasted_iota(jnp.int32, (CHUNK, CHUNK), 1) * CHUNK + mid
        results = []
        for c in batch:
            pieces = jnp.concatenate(split3(logbuf[:, rows_of(c)]), axis=0)
            token = lax.broadcasted_iota(jnp.int32, (CHUNK, CHUNK), 0) + c * CHUNK
            hit = ((token <= window) & (token > window - CHUNK)) | (window == 15 * CHUNK + mid)
            matrix = jnp.concatenate((sums[0], sums[1], sums[2], jnp.where(hit, 1.0, 0.0).astype(BF16)), axis=1)
            result = dot(pieces, matrix)
            results.append(result[:heads] + result[heads : 2 * heads] + result[2 * heads :])
        for c, result in zip(batch, results):
            centred = result[:, :CHUNK]
            values = []
            for value in (
                jnp.exp(-centred) * stepbuf[:, rows_of(c)],
                jnp.exp(centred),
                jnp.exp(before + result[:, CHUNK : 2 * CHUNK]),
            ):
                high = value.astype(BF16).astype(F32)
                values += [high, value - high]
            factors[c] = jnp.concatenate(values, axis=0).T.astype(BF16)
            before = before + result[:, 2 * CHUNK : 3 * CHUNK]
            windows = windows + result[:, 3 * CHUNK :]
        return before, windows

    none = jnp.zeros((heads, CHUNK), F32)
    _, windows = lax.fori_loop(0, chunks // BATCH, decays, (none, none))
    head_rows = jnp.exp(windows).T[:16]
    lam_row = jnp.concatenate(split3(head_rows[15:16]) + (jnp.zeros((1, LANES - 3 * heads), BF16),), axis=1)
    lam_tile = jnp.broadcast_to(lam_row.astype(F32), (part_rows, LANES)).astype(BF16)

    def put_lam(d, _):
        parts[d, TILES] = lam_tile
        return 0

    lax.fori_loop(0, ctx_size, put_lam, 0, unroll=4)
    row_at = lax.broadcasted_iota(jnp.int32, (16, heads), 0)
    head_rows = jnp.where(row_at == 14, skip_ref[...], head_rows)
    head_rows = dot(jnp.concatenate(split3(head_rows), axis=1), spread[...])
    for lane in range(groups * TILES):
        rows_ref[lane] = head_rows[:, lane * LANES : (lane + 1) * LANES]

    def part_copy(src, dst, to):
        return pltpu.make_async_remote_copy(
            src_ref=src, dst_ref=dst, send_sem=part_send.at[0], recv_sem=part_recv.at[0],
            device_id=(to, tp), device_id_type=MESH,
        )

    def start_copy(src, dst, to):
        return pltpu.make_async_remote_copy(
            src_ref=src, dst_ref=dst, send_sem=start_send.at[0], recv_sem=start_recv.at[mine],
            device_id=(to, tp), device_id_type=MESH,
        )

    def await_starts(g):
        def some(count):
            bytes_of = send.at[pl.ds(0, count)]
            pltpu.make_async_remote_copy(
                src_ref=bytes_of, dst_ref=bytes_of, send_sem=start_send.at[0], recv_sem=start_recv.at[g],
                device_id=(right, tp), device_id_type=MESH,
            ).wait_recv()

        pl.when(mine != g)(lambda: some(per_group))
        if per_group > 1:
            pl.when(mine == g)(lambda: some(per_group - 1))

    def ssq_copy(p, to):
        return pltpu.make_async_remote_copy(
            src_ref=ssq.at[p], dst_ref=ssq_recv.at[p, tp], send_sem=ssq_send.at[p],
            recv_sem=ssq_recv_sem.at[p], device_id=(me, to), device_id_type=MESH,
        )

    def all_ssq(p):
        others = ssq_recv.at[p, pl.ds(0, tp_size - 1)]
        return pltpu.make_async_remote_copy(
            src_ref=others, dst_ref=others, send_sem=ssq_send.at[p], recv_sem=ssq_recv_sem.at[p],
            device_id=(me, tp), device_id_type=MESH,
        )

    others = pl.ds(0, ctx_size - 1)
    all_parts = part_copy(parts.at[others], recv.at[others], right)

    for load in bc_loads:
        load.wait()

    bc_taps = [0.5 * convbc_ref[k : k + 1, :] for k in range(4)]

    def project(b):
        batch = [b * BATCH + k for k in range(BATCH)]
        blocks, moved = [], []
        for c in batch:
            rows = pl.ds(pl.multiple_of(c * CHUNK, CHUNK), CHUNK + HALO)
            blocks.append(jnp.concatenate((bcbuf[0, rows], bcbuf[1, rows]), axis=1))
        for block in blocks:
            moved.append(dot(shift_one[...], block))
        turned, c_rows = [], []
        for c, block, move in zip(batch, blocks, moved):
            half = bc_taps[3] * block[HALO:].astype(F32)
            for by in range(1, 4):
                half = half + bc_taps[3 - by] * move[(by - 1) * CHUNK : by * CHUNK]
            both = silu_of_half(half).astype(BF16)
            c_rows.append(both[:, n_state:])
            turned.append(both[:, :n_state].T)
            bt[c] = turned[-1]
            c_ref[c] = c_rows[-1]
        causal = lax.broadcasted_iota(jnp.int32, (CHUNK, CHUNK), 0) >= lax.broadcasted_iota(
            jnp.int32, (CHUNK, CHUNK), 1
        )
        scores = [dot(c_row, b_turned) for c_row, b_turned in zip(c_rows, turned)]
        for c, score in zip(batch, scores):
            scores_ref[c] = jnp.where(causal, score, 0.0).astype(BF16)

    batches = chunks // BATCH

    def project_step(k, _):
        project(batches - 1 - k)
        return 0

    lax.fori_loop(0, batches - 1, project_step, 0)

    def carry_through():
        all_parts.wait_recv()
        col = pl.multiple_of(mine * GROUP, GROUP)
        decay = recv[:, TILES].reshape(ctx_size * part_rows, LANES)[:, : 3 * heads]
        decay = dot(decay, spread[:, pl.ds(col, GROUP)])
        lam_wide[...] = decay.reshape(ctx_size, part_rows, GROUP)

        def step(d, running):
            for k in range(TILES):
                send[d, k] = running[:, k * LANES : (k + 1) * LANES].astype(BF16)
            arrived = jnp.concatenate([recv[d, k] for k in range(TILES)], axis=1)
            return lam_wide[d] * running + arrived.astype(F32)

        lax.fori_loop(0, ctx_size, step, jnp.zeros((part_rows, GROUP), F32), unroll=4)
        here = start_state.at[pl.ds(mine * TILES, TILES), pl.ds(my_row, part_rows)]
        start_state[pl.ds(mine * TILES, TILES), pl.ds(my_row, part_rows)] = send[me]

        def send_start(k):
            to = lax.rem(me + k, ctx_size)
            start_copy(send.at[to], here, to).start()

        each_other(ctx_size, send_start)

    def tap_sums(g, b):
        col = pl.ds(pl.multiple_of(g * GROUP, GROUP), GROUP)
        taps = [(0.5 * convx_ref[k : k + 1, col]).astype(BF16) for k in range(4)]
        shifts = jnp.concatenate([shift_all[by] for by in range(4)] + [shift_rim[...]], axis=1)

        def one(k):
            at = pl.multiple_of((b * BATCH + k) * CHUNK, CHUNK)
            block = wide(xbuf, g, pl.ds(at, CHUNK + HALO))
            terms = [block * taps[3 - by] for by in range(1, 4)]
            stacked = jnp.concatenate(
                [block[HALO:] * taps[3]] + [term[HALO:] for term in terms] + [term[:HALO] for term in terms], axis=0
            )
            return dot(shifts, stacked)

        return one

    def scale_batch(g, b, next_sums):
        factor = factors[pl.ds(b * BATCH, BATCH)].reshape(BATCH * CHUNK, 6 * heads)
        scales = dot(factor, wide(factor_map.at[0], g, slice(None)))
        scaled = []
        for k in range(BATCH):
            value = silu_of_half(ahead[k])
            ahead[k] = next_sums(k)
            put(xconv, g, (rows_of(b * BATCH + k),), value.astype(BF16))
            scaled.append((value * scales[k * CHUNK : (k + 1) * CHUNK]).astype(BF16))
            put(xs, g, (b * BATCH + k, slice(0, CHUNK)), scaled[-1])
        return scaled

    def leave(g):
        for r in range(per_group):
            for k in range(TILES):
                parts[carrier(g, r), k] = state[
                    r * part_rows : (r + 1) * part_rows, k * LANES : (k + 1) * LANES
                ].astype(BF16)

        def send_part(k):
            to = carrier(g, lax.rem(me // groups + k, per_group))
            part_copy(parts.at[to], recv.at[me], to).start()

        @pl.when(mine == g)
        def _():
            recv[me] = parts[me]

        @pl.when(mine != g)
        def _():
            send_part(0)

        if per_group > 1:
            each_other(per_group, send_part)

    later = batches - 1
    count = groups * later

    def later_at(u):
        return lax.div(u, later), lax.rem(u, later) + 1

    def forward(u, _):
        scale_batch(*later_at(u), tap_sums(*later_at(lax.rem(u + 1, count))))
        return 0

    for k in range(groups * TILES):
        x_load(k).wait()
    first_sums = tap_sums(*later_at(jnp.int32(0)))
    for k in range(BATCH):
        ahead[k] = first_sums(k)
    lax.fori_loop(0, count // 2, forward, 0)
    pl.semaphore_wait(barrier, ctx_size + tp_size - 2)
    for halo in halos:
        halo.start()
    lax.fori_loop(count // 2, count, forward, 0)

    for halo, rim, ref in zip(halos, (bc_rim, x_rim), (bcbuf, xbuf)):
        halo.wait_recv()
        for k in range(ref.shape[0]):
            before = rim[:, k * LANES : (k + 1) * LANES].astype(F32)
            ref[k, 0:HALO] = jnp.where(me > 0, before, 0.0).astype(BF16)
    project(0)
    first_sums = tap_sums(jnp.int32(0), 0)
    for k in range(BATCH):
        ahead[k] = first_sums(k)

    def settle(g, _):
        scaled = scale_batch(g, 0, tap_sums(lax.rem(g + 1, groups), 0))
        held = jnp.zeros((n_state, GROUP), F32)
        for c in range(chunks):
            value = scaled[c] if c < BATCH else wide(xs, g, c, slice(0, CHUNK))
            more = dot(bt[c], value)
            put(xs, g, (c, slice(CHUNK, CHUNK + n_state)), held.astype(BF16))
            held = wide(rows_ref, g, slice(c + 1, c + 2)) * (held + more)
        state[...] = held
        leave(g)
        return 0

    lax.fori_loop(0, groups, settle, 0)

    for k in range(groups * TILES):
        z_load(k).wait()

    def local(b, _):
        batch = [b * PAIR + k for k in range(PAIR)]
        factor = factors[pl.ds(b * PAIR, PAIR)].reshape(PAIR * CHUNK, 6 * heads)
        for g in range(groups):
            inner = [
                dot(
                    jnp.concatenate((scores_ref[c], c_ref[c]), axis=1),
                    wide(xs, g, c),
                )
                for c in batch
            ]
            scales = dot(factor, wide(factor_map.at[1], g, slice(None)))
            reaches = dot(factor, wide(factor_map.at[2], g, slice(None)))
            skip = wide(rows_ref, g, slice(14, 15))
            for k, c in enumerate(batch):
                part = slice(k * CHUNK, (k + 1) * CHUNK)
                gate = silu_of_half((wide(zbuf, g, rows_of(c)) * 0.5).astype(F32))
                skipped = skip * wide(xconv, g, rows_of(c)).astype(F32)
                put(local_ref, g, (rows_of(c),), (inner[k] * scales[part] + skipped) * gate)
                put(gate_ref, g, (rows_of(c),), (reaches[part] * gate).astype(BF16))
        return 0

    def local_step(b, _):
        pl.when(b == lax.min(chunks // PAIR // 3 + mine, chunks // PAIR - 1))(carry_through)
        return local(b, 0)

    lax.fori_loop(0, chunks // PAIR, local_step, 0)

    def finish(p, g):
        batch = [p * BATCH + k for k in range(BATCH)]
        c_rows = c_ref[pl.ds(p * BATCH, BATCH)].reshape(BATCH * CHUNK, n_state)
        carried = dot(c_rows, wide(start_state, g, slice(None)))
        gain = wide(gain_ref, g)
        totals = []
        for k, c in enumerate(batch):
            reach = wide(gate_ref, g, rows_of(c)).astype(F32)
            gated = wide(local_ref, g, rows_of(c)) + reach * carried[k * CHUNK : (k + 1) * CHUNK]
            put(local_ref, g, (rows_of(c),), gated * gain)
            both = gated * gated
            total = both[:, :LANES]
            for lane in range(LANES, GROUP, LANES):
                total = total + both[:, lane : lane + LANES]
            totals.append(total)
        return batch, totals

    def finish_group(g, _):
        await_starts(g)

        def step(p, _):
            for c, total in zip(*finish(p, g)):
                squares[c] = jnp.where(g == 0, 0.0, squares[c]) + total
            return 0

        lax.fori_loop(0, batches, step, 0)
        return 0

    lax.fori_loop(0, groups - 1, finish_group, 0)
    await_starts(groups - 1)

    def piece(p, _):
        for k, (c, total) in enumerate(zip(*finish(p, groups - 1))):
            ssq[p, k : k + 1, :] = jnp.sum((squares[c] + total).T, axis=0, keepdims=True)
        ssq[p, BATCH:, :] = jnp.zeros((8 - BATCH, LANES), F32)
        ssq_recv[p, tp] = ssq[p]
        each_other(tp_size, lambda k: ssq_copy(p, lax.rem(tp + k, tp_size)).start())
        return 0

    lax.fori_loop(0, batches, piece, 0)

    for halo in halos:
        halo.wait_send()
    all_parts.wait_send()
    start_copy(send.at[others], send.at[others], right).wait_send()

    def norm(b, _):
        all_ssq(b).wait_recv()
        mean = jnp.sum(ssq_recv[b], axis=0) * (1.0 / (channels * tp_size))
        inverse = lax.rsqrt(mean + 1e-5)
        for k in range(BATCH):
            at = rows_of(b * BATCH + k)
            column = jnp.broadcast_to(inverse[k : k + 1], (CHUNK, CHUNK)).T
            for lane in range(groups * TILES):
                here = slice(lane * LANES, (lane + 1) * LANES)
                out_ref[at, here] = (local_ref[lane, at] * column).astype(BF16)
        return 0

    lax.fori_loop(0, batches, norm, 0)
    for b in range(batches):
        all_ssq(b).wait_send()


def per_device(
    x_raw, bc_raw, z_gate, conv_x, conv_bc, step_size, log_decay, skip_scale, norm_gain, *, ctx_size, tp_size
):
    length, channels = x_raw.shape
    heads = step_size.shape[1]
    head_dim = channels // heads
    n_state = bc_raw.shape[1] // 2
    chunks = length // CHUNK
    groups = channels // GROUP
    lanes = channels // LANES
    part_rows = n_state * groups // ctx_size
    in_hbm = pl.BlockSpec(memory_space=pltpu.HBM)
    vmem = pltpu.VMEM
    dma = pltpu.SemaphoreType.DMA
    return pl.pallas_call(
        functools.partial(mixer, ctx_size, tp_size, head_dim),
        out_shape=pltpu.VMEM((length, channels), BF16),
        in_specs=[in_hbm] * 9,
        out_specs=pl.BlockSpec(memory_space=pltpu.VMEM),
        scratch_shapes=[
            vmem((lanes, length + HALO, LANES), BF16),
            vmem((2, length + HALO, n_state), BF16),
            vmem((lanes, length, LANES), BF16),
            vmem((HALO, channels), BF16),
            vmem((HALO, 2 * n_state), BF16),
            vmem((heads, length), F32),
            vmem((heads, length), F32),
            vmem((4, channels), F32),
            vmem((4, 2 * n_state), F32),
            vmem((1, heads), F32),
            vmem((lanes, 1, LANES), F32),
            vmem((3 * heads, channels), BF16),
            vmem((3, lanes, 6 * heads, LANES), BF16),
            vmem((3 * CHUNK, CHUNK + HALO), BF16),
            vmem((4, CHUNK, CHUNK), BF16),
            vmem((CHUNK, 3 * HALO), BF16),
            vmem((3, CHUNK, CHUNK), BF16),
            vmem((chunks, CHUNK, 6 * heads), BF16),
            vmem((lanes, 16, LANES), F32),
            vmem((chunks, CHUNK, CHUNK), BF16),
            vmem((chunks, CHUNK, n_state), BF16),
            vmem((chunks, n_state, CHUNK), BF16),
            vmem((lanes, length, LANES), BF16),
            vmem((lanes, chunks, CHUNK + n_state, LANES), BF16),
            vmem((n_state, GROUP), F32),
            vmem((ctx_size, TILES + 1, part_rows, LANES), BF16),
            vmem((ctx_size, TILES + 1, part_rows, LANES), BF16),
            vmem((ctx_size, part_rows, GROUP), F32),
            vmem((ctx_size, TILES, part_rows, LANES), BF16),
            vmem((lanes, n_state, LANES), BF16),
            vmem((BATCH, CHUNK, GROUP), F32),
            vmem((lanes, length, LANES), F32),
            vmem((lanes, length, LANES), BF16),
            vmem((chunks, CHUNK, LANES), F32),
            vmem((chunks // BATCH, 8, LANES), F32),
            vmem((chunks // BATCH, tp_size, 8, LANES), F32),
            dma((7 + 3 * lanes,)),
            dma((2,)),
            dma((2,)),
            dma((1,)),
            dma((1,)),
            dma((1,)),
            dma((groups,)),
            dma((chunks // BATCH,)),
            dma((chunks // BATCH,)),
        ],
        compiler_params=pltpu.CompilerParams(
            collective_id=0, has_side_effects=True, vmem_limit_bytes=56 * 1024 * 1024
        ),
        name="mixer",
    )(
        x_raw, bc_raw, z_gate, conv_x, conv_bc, step_size.T, log_decay.T,
        skip_scale.reshape(1, heads), norm_gain.reshape(1, channels),
    )


def solution(mesh):
    sizes = dict(mesh.shape)
    return jax.shard_map(
        functools.partial(per_device, ctx_size=sizes["ctx"], tp_size=sizes["tp"]),
        mesh=mesh,
        in_specs=(
            P("ctx", "tp"),
            P("ctx", None),
            P("ctx", "tp"),
            P(None, "tp"),
            P(),
            P("ctx", "tp"),
            P("ctx", "tp"),
            P("tp"),
            P("tp"),
        ),
        out_specs=P("ctx", "tp"),
        check_vma=False,
    )
```

```python
import functools

import jax
import jax.numpy as jnp
from jax import lax
from jax.experimental import pallas as pl
from jax.experimental.pallas import tpu as pltpu
from jax.sharding import PartitionSpec as P

F32 = jnp.float32
BF16 = jnp.bfloat16
MESH = pl.DeviceIdType.MESH
CHUNK = 128
LANES = 128
GROUP = 256
TILES = GROUP // LANES
HALO = 16
BATCH = 4
PAIR = 2


def split3(value):
    high = value.astype(BF16)
    rest = value - high.astype(F32)
    mid = rest.astype(BF16)
    return high, mid, (rest - mid.astype(F32)).astype(BF16)


def silu_of_half(half):
    return half * jnp.tanh(half) + half


def dot(left, right):
    return jnp.dot(left, right, preferred_element_type=F32)


def each_other(size, fn):
    count = size - 1
    unroll = next(n for n in (6, 5, 4, 3, 2, 1) if (count - 1) % n == 0)

    def step(k, _):
        fn(k)
        return 0

    if count > 1:
        lax.fori_loop(1, count, step, 0, unroll=unroll)
    fn(count)


def mixer(
    ctx_size, tp_size, head_dim,
    x_hbm, bc_hbm, z_hbm, convx_hbm, convbc_hbm, step_hbm, log_hbm, skip_hbm, gain_hbm,
    out_ref,
    xbuf, bcbuf, zbuf, x_rim, bc_rim, stepbuf, logbuf, convx_ref, convbc_ref, skip_ref, gain_ref,
    spread, factor_map, shift_one, shift_all, shift_rim, sums, factors, rows_ref,
    scores_ref, c_ref, bt, xconv, xs, state, parts, recv, lam_wide, send, start_state,
    ahead, local_ref, gate_ref, squares, ssq, ssq_recv,
    load_sem, halo_send, halo_recv, part_send, part_recv, start_send, start_recv, ssq_send, ssq_recv_sem,
):
    length, channels = x_hbm.shape
    heads = step_hbm.shape[0]
    chunks = length // CHUNK
    groups = channels // GROUP
    n_state = bt.shape[1]
    part_rows = parts.shape[2]
    per_group = ctx_size // groups
    mid = CHUNK // 2 - 1
    me = lax.axis_index("ctx")
    tp = lax.axis_index("tp")
    mine = lax.rem(me // 2 + me // 8, 2) * 2 + lax.rem(me, 2)
    my_row = pl.multiple_of((me // groups) * part_rows, part_rows)

    def carrier(g, r):
        return r * groups + lax.rem(g // 2 + r // 2, 2) * 2 + lax.rem(g, 2)

    def wide(ref, g, *at):
        return jnp.concatenate([ref[(g * TILES + k, *at)] if at else ref[g * TILES + k] for k in range(TILES)], axis=-1)

    def put(ref, g, at, value):
        for k in range(TILES):
            ref[(g * TILES + k, *at)] = value[:, k * LANES : (k + 1) * LANES]

    def rows_of(c):
        return pl.ds(pl.multiple_of(c * CHUNK, CHUNK), CHUNK)

    small_loads = [
        pltpu.make_async_copy(src, dst, load_sem.at[k])
        for k, (src, dst) in enumerate(
            (
                (log_hbm, logbuf),
                (step_hbm, stepbuf),
                (skip_hbm, skip_ref),
                (convbc_hbm, convbc_ref),
                (convx_hbm, convx_ref),
                *[
                    (gain_hbm.at[:, pl.ds(k * LANES, LANES)], gain_ref.at[k])
                    for k in range(groups * TILES)
                ],
            )
        )
    ]
    at_bc = len(small_loads)
    bc_loads = [
        pltpu.make_async_copy(
            bc_hbm.at[:, pl.ds(k * LANES, LANES)], bcbuf.at[k, pl.ds(HALO, length)], load_sem.at[at_bc + k]
        )
        for k in range(2)
    ]

    def x_load(k):
        col = pl.ds(pl.multiple_of(k * LANES, LANES), LANES)
        return pltpu.make_async_copy(x_hbm.at[:, col], xbuf.at[k, pl.ds(HALO, length)], load_sem.at[at_bc + 2 + k])

    def z_load(k):
        col = pl.ds(pl.multiple_of(k * LANES, LANES), LANES)
        return pltpu.make_async_copy(
            z_hbm.at[:, col], zbuf.at[k], load_sem.at[at_bc + 2 + groups * TILES + k]
        )

    for load in small_loads + bc_loads:
        load.start()
    for k in range(groups * TILES):
        x_load(k).start()
    for k in range(groups * TILES):
        z_load(k).start()

    barrier = pltpu.get_barrier_semaphore()

    def greet_ctx(k):
        pl.semaphore_signal(barrier, inc=1, device_id=(lax.rem(me + ctx_size - k, ctx_size), tp), device_id_type=MESH)

    def greet_tp(k):
        pl.semaphore_signal(barrier, inc=1, device_id=(me, lax.rem(tp + k, tp_size)), device_id_type=MESH)

    each_other(ctx_size, greet_ctx)
    each_other(tp_size, greet_tp)

    right = lax.rem(me + 1, ctx_size)

    def halo_copy(src, dst, at):
        return pltpu.make_async_remote_copy(
            src_ref=src.at[pl.ds(length - HALO, HALO)], dst_ref=dst, send_sem=halo_send.at[at],
            recv_sem=halo_recv.at[at], device_id=(right, tp), device_id_type=MESH,
        )

    halos = [halo_copy(bc_hbm, bc_rim, 0), halo_copy(x_hbm, x_rim, 1)]
    s_at = lax.broadcasted_iota(jnp.int32, (CHUNK, CHUNK), 0)
    t_at = lax.broadcasted_iota(jnp.int32, (CHUNK, CHUNK), 1)
    upto = jnp.where(s_at <= t_at, 1.0, 0.0)
    sums[0] = (upto - jnp.where(s_at <= mid, 1.0, 0.0)).astype(BF16)
    sums[1] = upto.astype(BF16)
    sums[2] = jnp.ones((CHUNK, CHUNK), BF16)

    head_at = lax.broadcasted_iota(jnp.int32, (heads, channels), 0)
    channel_at = lax.broadcasted_iota(jnp.int32, (heads, channels), 1)
    first = head_at * head_dim
    one_map = jnp.where((channel_at >= first) & (channel_at < first + head_dim), 1.0, 0.0).astype(BF16)
    factor_map[...] = jnp.zeros_like(factor_map)
    for k in range(3):
        spread[k * heads : (k + 1) * heads, :] = one_map
        for term in range(2):
            row = (2 * k + term) * heads
            for lane in range(groups * TILES):
                factor_map[k, lane, row : row + heads, :] = one_map[:, lane * LANES : (lane + 1) * LANES]

    def shift(by, width, before):
        to = lax.broadcasted_iota(jnp.int32, (CHUNK, width), 0)
        at = lax.broadcasted_iota(jnp.int32, (CHUNK, width), 1)
        return jnp.where(to + (before - by) == at, 1.0, 0.0).astype(BF16)

    for by in range(1, 4):
        shift_all[by - 1] = shift(by, CHUNK, 0)
        shift_one[(by - 1) * CHUNK : by * CHUNK, :] = shift(by, CHUNK + HALO, HALO)
    halo_to = lax.broadcasted_iota(jnp.int32, (CHUNK, 3 * HALO), 0)
    halo_at = lax.broadcasted_iota(jnp.int32, (CHUNK, 3 * HALO), 1)
    halo_hit = halo_to < 0
    for by in range(1, 4):
        inside = (halo_at >= (by - 1) * HALO) & (halo_at < by * HALO)
        halo_hit = halo_hit | ((halo_to + (by * HALO - by) == halo_at) & inside)
    shift_rim[...] = jnp.where(halo_hit, 1.0, 0.0).astype(BF16)

    for load in small_loads:
        load.wait()

    def decays(b, carry):
        before, windows = carry
        batch = [b * BATCH + k for k in range(BATCH)]
        window = lax.broadcasted_iota(jnp.int32, (CHUNK, CHUNK), 1) * CHUNK + mid
        results = []
        for c in batch:
            pieces = jnp.concatenate(split3(logbuf[:, rows_of(c)]), axis=0)
            token = lax.broadcasted_iota(jnp.int32, (CHUNK, CHUNK), 0) + c * CHUNK
            hit = ((token <= window) & (token > window - CHUNK)) | (window == 15 * CHUNK + mid)
            matrix = jnp.concatenate((sums[0], sums[1], sums[2], jnp.where(hit, 1.0, 0.0).astype(BF16)), axis=1)
            result = dot(pieces, matrix)
            results.append(result[:heads] + result[heads : 2 * heads] + result[2 * heads :])
        for c, result in zip(batch, results):
            centred = result[:, :CHUNK]
            values = []
            for value in (
                jnp.exp(-centred) * stepbuf[:, rows_of(c)],
                jnp.exp(centred),
                jnp.exp(before + result[:, CHUNK : 2 * CHUNK]),
            ):
                high = value.astype(BF16).astype(F32)
                values += [high, value - high]
            factors[c] = jnp.concatenate(values, axis=0).T.astype(BF16)
            before = before + result[:, 2 * CHUNK : 3 * CHUNK]
            windows = windows + result[:, 3 * CHUNK :]
        return before, windows

    none = jnp.zeros((heads, CHUNK), F32)
    _, windows = lax.fori_loop(0, chunks // BATCH, decays, (none, none), unroll=True)
    head_rows = jnp.exp(windows).T[:16]
    lam_row = jnp.concatenate(split3(head_rows[15:16]) + (jnp.zeros((1, LANES - 3 * heads), BF16),), axis=1)
    lam_tile = jnp.broadcast_to(lam_row.astype(F32), (part_rows, LANES)).astype(BF16)

    def put_lam(d, _):
        parts[d, TILES] = lam_tile
        return 0

    lax.fori_loop(0, ctx_size, put_lam, 0, unroll=4)
    row_at = lax.broadcasted_iota(jnp.int32, (16, heads), 0)
    head_rows = jnp.where(row_at == 14, skip_ref[...], head_rows)
    head_rows = dot(jnp.concatenate(split3(head_rows), axis=1), spread[...])
    for lane in range(groups * TILES):
        rows_ref[lane] = head_rows[:, lane * LANES : (lane + 1) * LANES]

    def part_copy(src, dst, to):
        return pltpu.make_async_remote_copy(
            src_ref=src, dst_ref=dst, send_sem=part_send.at[0], recv_sem=part_recv.at[0],
            device_id=(to, tp), device_id_type=MESH,
        )

    def start_copy(src, dst, to):
        return pltpu.make_async_remote_copy(
            src_ref=src, dst_ref=dst, send_sem=start_send.at[0], recv_sem=start_recv.at[mine],
            device_id=(to, tp), device_id_type=MESH,
        )

    def await_starts(g):
        def some(count):
            bytes_of = send.at[pl.ds(0, count)]
            pltpu.make_async_remote_copy(
                src_ref=bytes_of, dst_ref=bytes_of, send_sem=start_send.at[0], recv_sem=start_recv.at[g],
                device_id=(right, tp), device_id_type=MESH,
            ).wait_recv()

        pl.when(mine != g)(lambda: some(per_group))
        if per_group > 1:
            pl.when(mine == g)(lambda: some(per_group - 1))

    def ssq_copy(p, to):
        return pltpu.make_async_remote_copy(
            src_ref=ssq.at[p], dst_ref=ssq_recv.at[p, tp], send_sem=ssq_send.at[p],
            recv_sem=ssq_recv_sem.at[p], device_id=(me, to), device_id_type=MESH,
        )

    def all_ssq(p):
        others = ssq_recv.at[p, pl.ds(0, tp_size - 1)]
        return pltpu.make_async_remote_copy(
            src_ref=others, dst_ref=others, send_sem=ssq_send.at[p], recv_sem=ssq_recv_sem.at[p],
            device_id=(me, tp), device_id_type=MESH,
        )

    others = pl.ds(0, ctx_size - 1)
    all_parts = part_copy(parts.at[others], recv.at[others], right)

    for load in bc_loads:
        load.wait()

    bc_taps = [0.5 * convbc_ref[k : k + 1, :] for k in range(4)]

    def project(side, b):
        part = slice(side * n_state, (side + 1) * n_state)
        blocks = [
            bcbuf[side, pl.ds(pl.multiple_of((b * BATCH + k) * CHUNK, CHUNK), CHUNK + HALO)] for k in range(BATCH)
        ]
        moved = [dot(shift_one[...], block) for block in blocks]
        results = []
        for block, move in zip(blocks, moved):
            half = bc_taps[3][:, part] * block[HALO:].astype(F32)
            for by in range(1, 4):
                half = half + bc_taps[3 - by][:, part] * move[(by - 1) * CHUNK : by * CHUNK]
            results.append(silu_of_half(half).astype(BF16))
        return results

    def project_b(b):
        for k, value in enumerate(project(0, b)):
            bt[b * BATCH + k] = value.T

    def project_c(b, _):
        values = project(1, b)
        causal = lax.broadcasted_iota(jnp.int32, (CHUNK, CHUNK), 0) >= lax.broadcasted_iota(
            jnp.int32, (CHUNK, CHUNK), 1
        )
        scores = [dot(value, bt[b * BATCH + k]) for k, value in enumerate(values)]
        for k, value in enumerate(values):
            c_ref[b * BATCH + k] = value
            scores_ref[b * BATCH + k] = jnp.where(causal, scores[k], 0.0).astype(BF16)
        return 0

    batches = chunks // BATCH

    def project_step(k, _):
        project_b(batches - 1 - k)
        return 0

    lax.fori_loop(0, batches - 1, project_step, 0, unroll=True)

    def carry_through():
        all_parts.wait_recv()
        col = pl.multiple_of(mine * GROUP, GROUP)
        decay = recv[:, TILES].reshape(ctx_size * part_rows, LANES)[:, : 3 * heads]
        decay = dot(decay, spread[:, pl.ds(col, GROUP)])
        lam_wide[...] = decay.reshape(ctx_size, part_rows, GROUP)

        def step(d, running):
            for k in range(TILES):
                send[d, k] = running[:, k * LANES : (k + 1) * LANES].astype(BF16)
            arrived = jnp.concatenate([recv[d, k] for k in range(TILES)], axis=1)
            return lam_wide[d] * running + arrived.astype(F32)

        lax.fori_loop(0, ctx_size, step, jnp.zeros((part_rows, GROUP), F32), unroll=4)
        here = start_state.at[pl.ds(mine * TILES, TILES), pl.ds(my_row, part_rows)]
        start_state[pl.ds(mine * TILES, TILES), pl.ds(my_row, part_rows)] = send[me]

        def send_start(k):
            far_first = lax.rem(k + ctx_size // 3, ctx_size - 1) + 1
            to = lax.rem(me + far_first, ctx_size)
            start_copy(send.at[to], here, to).start()

        each_other(ctx_size, send_start)

    def tap_sums(g, b):
        col = pl.ds(pl.multiple_of(g * GROUP, GROUP), GROUP)
        taps = [(0.5 * convx_ref[k : k + 1, col]).astype(BF16) for k in range(3)]
        shifts = jnp.concatenate([shift_all[by] for by in range(3)] + [shift_rim[...]], axis=1)

        def one(k):
            at = pl.multiple_of((b * BATCH + k) * CHUNK, CHUNK)
            block = wide(xbuf, g, pl.ds(at, CHUNK + HALO))
            terms = [block * taps[3 - by] for by in range(1, 4)]
            stacked = jnp.concatenate([term[HALO:] for term in terms] + [term[:HALO] for term in terms], axis=0)
            return dot(shifts, stacked) + 0.5 * convx_ref[3:4, col] * block[HALO:].astype(F32)

        return one

    def scale_batch(g, b, next_sums):
        factor = factors[pl.ds(b * BATCH, BATCH)].reshape(BATCH * CHUNK, 6 * heads)
        scales = dot(factor, wide(factor_map.at[0], g, slice(None)))
        scaled = []
        for k in range(BATCH):
            value = silu_of_half(ahead[k])
            ahead[k] = next_sums(k)
            put(xconv, g, (rows_of(b * BATCH + k),), value.astype(BF16))
            scaled.append((value * scales[k * CHUNK : (k + 1) * CHUNK]).astype(BF16))
            put(xs, g, (b * BATCH + k, slice(0, CHUNK)), scaled[-1])
        return scaled

    def leave(g):
        for r in range(per_group):
            for k in range(TILES):
                parts[carrier(g, r), k] = state[
                    r * part_rows : (r + 1) * part_rows, k * LANES : (k + 1) * LANES
                ].astype(BF16)

        def send_part(k):
            to = carrier(g, lax.rem(me // groups + k, per_group))
            part_copy(parts.at[to], recv.at[me], to).start()

        @pl.when(mine == g)
        def _():
            recv[me] = parts[me]

        @pl.when(mine != g)
        def _():
            send_part(0)

        if per_group > 1:
            each_other(per_group, send_part)

    later = batches - 1
    count = groups * later

    def later_at(u):
        return lax.div(u, later), lax.rem(u, later) + 1

    def forward(u, _):
        scale_batch(*later_at(u), tap_sums(*later_at(lax.rem(u + 1, count))))
        return 0

    for k in range(groups * TILES):
        x_load(k).wait()
    first_sums = tap_sums(*later_at(jnp.int32(0)))
    for k in range(BATCH):
        ahead[k] = first_sums(k)
    lax.fori_loop(0, count // 2, forward, 0, unroll=2)
    pl.semaphore_wait(barrier, ctx_size + tp_size - 2)
    for halo in halos:
        halo.start()
    lax.fori_loop(count // 2, count, forward, 0, unroll=2)

    for halo, rim, ref in zip(halos, (bc_rim, x_rim), (bcbuf, xbuf)):
        halo.wait_recv()
        for k in range(ref.shape[0]):
            before = rim[:, k * LANES : (k + 1) * LANES].astype(F32)
            ref[k, 0:HALO] = jnp.where(me > 0, before, 0.0).astype(BF16)
    project_b(0)
    first_sums = tap_sums(jnp.int32(0), 0)
    for k in range(BATCH):
        ahead[k] = first_sums(k)

    def settle(g, _):
        scaled = scale_batch(g, 0, tap_sums(lax.rem(g + 1, groups), 0))
        held = jnp.zeros((n_state, GROUP), F32)
        for c in range(chunks):
            value = scaled[c] if c < BATCH else wide(xs, g, c, slice(0, CHUNK))
            more = dot(bt[c], value)
            put(xs, g, (c, slice(CHUNK, CHUNK + n_state)), held.astype(BF16))
            held = wide(rows_ref, g, slice(c + 1, c + 2)) * (held + more)
        state[...] = held
        leave(g)
        return 0

    lax.fori_loop(0, groups, settle, 0)

    lax.fori_loop(0, batches, project_c, 0)
    for k in range(groups * TILES):
        z_load(k).wait()

    def local(b, _):
        batch = [b * PAIR + k for k in range(PAIR)]
        factor = factors[pl.ds(b * PAIR, PAIR)].reshape(PAIR * CHUNK, 6 * heads)
        for g in range(groups):
            inner = [
                dot(
                    jnp.concatenate((scores_ref[c], c_ref[c]), axis=1),
                    wide(xs, g, c),
                )
                for c in batch
            ]
            scales = dot(factor, wide(factor_map.at[1], g, slice(None)))
            reaches = dot(factor, wide(factor_map.at[2], g, slice(None)))
            skip = wide(rows_ref, g, slice(14, 15))
            for k, c in enumerate(batch):
                part = slice(k * CHUNK, (k + 1) * CHUNK)
                gate = silu_of_half((wide(zbuf, g, rows_of(c)) * 0.5).astype(F32))
                skipped = skip * wide(xconv, g, rows_of(c)).astype(F32)
                put(local_ref, g, (rows_of(c),), (inner[k] * scales[part] + skipped) * gate)
                put(gate_ref, g, (rows_of(c),), (reaches[part] * gate).astype(BF16))
        return 0

    def local_step(b, _):
        pl.when(b == lax.min(chunks // PAIR // 3 + mine, chunks // PAIR - 1))(carry_through)
        return local(b, 0)

    lax.fori_loop(0, chunks // PAIR, local_step, 0)

    def finish(p, g):
        batch = [p * BATCH + k for k in range(BATCH)]
        c_rows = c_ref[pl.ds(p * BATCH, BATCH)].reshape(BATCH * CHUNK, n_state)
        carried = dot(c_rows, wide(start_state, g, slice(None)))
        gain = wide(gain_ref, g)
        totals = []
        for k, c in enumerate(batch):
            reach = wide(gate_ref, g, rows_of(c)).astype(F32)
            gated = wide(local_ref, g, rows_of(c)) + reach * carried[k * CHUNK : (k + 1) * CHUNK]
            put(local_ref, g, (rows_of(c),), gated * gain)
            both = gated * gated
            total = both[:, :LANES]
            for lane in range(LANES, GROUP, LANES):
                total = total + both[:, lane : lane + LANES]
            totals.append(total)
        return batch, totals

    def finish_group(g, _):
        await_starts(g)

        def step(p, _):
            for c, total in zip(*finish(p, g)):
                squares[c] = jnp.where(g == 0, 0.0, squares[c]) + total
            return 0

        lax.fori_loop(0, batches, step, 0)
        return 0

    lax.fori_loop(0, groups - 1, finish_group, 0)
    await_starts(groups - 1)

    def piece(p, _):
        for k, (c, total) in enumerate(zip(*finish(p, groups - 1))):
            ssq[p, k : k + 1, :] = jnp.sum((squares[c] + total).T, axis=0, keepdims=True)
        ssq[p, BATCH:, :] = jnp.zeros((8 - BATCH, LANES), F32)
        ssq_recv[p, tp] = ssq[p]
        each_other(
            tp_size, lambda k: ssq_copy(p, lax.rem(tp + lax.rem(k + 1, tp_size - 1) + 1, tp_size)).start()
        )
        return 0

    lax.fori_loop(0, batches, piece, 0)

    for halo in halos:
        halo.wait_send()
    all_parts.wait_send()
    start_copy(send.at[others], send.at[others], right).wait_send()

    def norm(b, _):
        all_ssq(b).wait_recv()
        mean = jnp.sum(ssq_recv[b], axis=0) * (1.0 / (channels * tp_size))
        inverse = lax.rsqrt(mean + 1e-5)
        for k in range(BATCH):
            at = rows_of(b * BATCH + k)
            column = jnp.broadcast_to(inverse[k : k + 1], (CHUNK, CHUNK)).T
            for lane in range(groups * TILES):
                here = slice(lane * LANES, (lane + 1) * LANES)
                out_ref[at, here] = (local_ref[lane, at] * column).astype(BF16)
        return 0

    lax.fori_loop(0, batches, norm, 0)
    for b in range(batches):
        all_ssq(b).wait_send()


def per_device(
    x_raw, bc_raw, z_gate, conv_x, conv_bc, step_size, log_decay, skip_scale, norm_gain, *, ctx_size, tp_size
):
    length, channels = x_raw.shape
    heads = step_size.shape[1]
    head_dim = channels // heads
    n_state = bc_raw.shape[1] // 2
    chunks = length // CHUNK
    groups = channels // GROUP
    lanes = channels // LANES
    part_rows = n_state * groups // ctx_size
    in_hbm = pl.BlockSpec(memory_space=pltpu.HBM)
    vmem = pltpu.VMEM
    dma = pltpu.SemaphoreType.DMA
    return pl.pallas_call(
        functools.partial(mixer, ctx_size, tp_size, head_dim),
        out_shape=pltpu.VMEM((length, channels), BF16),
        in_specs=[in_hbm] * 9,
        out_specs=pl.BlockSpec(memory_space=pltpu.VMEM),
        scratch_shapes=[
            vmem((lanes, length + HALO, LANES), BF16),
            vmem((2, length + HALO, n_state), BF16),
            vmem((lanes, length, LANES), BF16),
            vmem((HALO, channels), BF16),
            vmem((HALO, 2 * n_state), BF16),
            vmem((heads, length), F32),
            vmem((heads, length), F32),
            vmem((4, channels), F32),
            vmem((4, 2 * n_state), F32),
            vmem((1, heads), F32),
            vmem((lanes, 1, LANES), F32),
            vmem((3 * heads, channels), BF16),
            vmem((3, lanes, 6 * heads, LANES), BF16),
            vmem((3 * CHUNK, CHUNK + HALO), BF16),
            vmem((3, CHUNK, CHUNK), BF16),
            vmem((CHUNK, 3 * HALO), BF16),
            vmem((3, CHUNK, CHUNK), BF16),
            vmem((chunks, CHUNK, 6 * heads), BF16),
            vmem((lanes, 16, LANES), F32),
            vmem((chunks, CHUNK, CHUNK), BF16),
            vmem((chunks, CHUNK, n_state), BF16),
            vmem((chunks, n_state, CHUNK), BF16),
            vmem((lanes, length, LANES), BF16),
            vmem((lanes, chunks, CHUNK + n_state, LANES), BF16),
            vmem((n_state, GROUP), F32),
            vmem((ctx_size, TILES + 1, part_rows, LANES), BF16),
            vmem((ctx_size, TILES + 1, part_rows, LANES), BF16),
            vmem((ctx_size, part_rows, GROUP), F32),
            vmem((ctx_size, TILES, part_rows, LANES), BF16),
            vmem((lanes, n_state, LANES), BF16),
            vmem((BATCH, CHUNK, GROUP), F32),
            vmem((lanes, length, LANES), F32),
            vmem((lanes, length, LANES), BF16),
            vmem((chunks, CHUNK, LANES), F32),
            vmem((chunks // BATCH, 8, LANES), F32),
            vmem((chunks // BATCH, tp_size, 8, LANES), F32),
            dma((7 + 3 * lanes,)),
            dma((2,)),
            dma((2,)),
            dma((1,)),
            dma((1,)),
            dma((1,)),
            dma((groups,)),
            dma((chunks // BATCH,)),
            dma((chunks // BATCH,)),
        ],
        compiler_params=pltpu.CompilerParams(
            collective_id=0, has_side_effects=True, vmem_limit_bytes=56 * 1024 * 1024
        ),
        name="mixer",
    )(
        x_raw, bc_raw, z_gate, conv_x, conv_bc, step_size.T, log_decay.T,
        skip_scale.reshape(1, heads), norm_gain.reshape(1, channels),
    )


def solution(mesh):
    sizes = dict(mesh.shape)
    return jax.shard_map(
        functools.partial(per_device, ctx_size=sizes["ctx"], tp_size=sizes["tp"]),
        mesh=mesh,
        in_specs=(
            P("ctx", "tp"),
            P("ctx", None),
            P("ctx", "tp"),
            P(None, "tp"),
            P(),
            P("ctx", "tp"),
            P("ctx", "tp"),
            P("tp"),
            P("tp"),
        ),
        out_specs=P("ctx", "tp"),
        check_vma=False,
    )
```

```python
import functools

import jax
import jax.numpy as jnp
from jax import lax
from jax.experimental import pallas as pl
from jax.experimental.pallas import tpu as pltpu
from jax.sharding import PartitionSpec as P

F32 = jnp.float32
BF16 = jnp.bfloat16
MESH = pl.DeviceIdType.MESH
CHUNK = 128
LANES = 128
GROUP = 256
TILES = GROUP // LANES
HALO = 16
BATCH = 4
PAIR = 2


def split3(value):
    high = value.astype(BF16)
    rest = value - high.astype(F32)
    mid = rest.astype(BF16)
    return high, mid, (rest - mid.astype(F32)).astype(BF16)


def silu_of_half(half):
    return half * jnp.tanh(half) + half


def dot(left, right):
    return jnp.dot(left, right, preferred_element_type=F32)


def each_other(size, fn):
    count = size - 1
    unroll = next(n for n in (6, 5, 4, 3, 2, 1) if (count - 1) % n == 0)

    def step(k, _):
        fn(k)
        return 0

    if count > 1:
        lax.fori_loop(1, count, step, 0, unroll=unroll)
    fn(count)


def mixer(
    ctx_size, tp_size, head_dim,
    x_hbm, bc_hbm, z_hbm, convx_hbm, convbc_hbm, step_hbm, log_hbm, skip_hbm, gain_hbm,
    out_ref,
    xbuf, bcbuf, zbuf, x_rim, bc_rim, stepbuf, logbuf, convx_ref, convbc_ref, skip_ref, gain_ref,
    spread, factor_map, shift_one, shift_all, shift_rim, sums, factors, rows_ref,
    scores_ref, c_ref, bt, xconv, xs, state, parts, recv, lam_wide, send, start_state,
    ahead, local_ref, gate_ref, squares, ssq, ssq_recv,
    load_sem, halo_send, halo_recv, part_send, part_recv, start_send, start_recv, ssq_send, ssq_recv_sem,
):
    length, channels = x_hbm.shape
    heads = step_hbm.shape[0]
    chunks = length // CHUNK
    groups = channels // GROUP
    n_state = bt.shape[1]
    part_rows = parts.shape[2]
    per_group = ctx_size // groups
    mid = CHUNK // 2 - 1
    me = lax.axis_index("ctx")
    tp = lax.axis_index("tp")
    mine = lax.rem(me // 2 + me // 8, 2) * 2 + lax.rem(me, 2)
    my_row = pl.multiple_of((me // groups) * part_rows, part_rows)

    def carrier(g, r):
        return r * groups + lax.rem(g // 2 + r // 2, 2) * 2 + lax.rem(g, 2)

    def wide(ref, g, *at):
        return jnp.concatenate([ref[(g * TILES + k, *at)] if at else ref[g * TILES + k] for k in range(TILES)], axis=-1)

    def put(ref, g, at, value):
        for k in range(TILES):
            ref[(g * TILES + k, *at)] = value[:, k * LANES : (k + 1) * LANES]

    def rows_of(c):
        return pl.ds(pl.multiple_of(c * CHUNK, CHUNK), CHUNK)

    small_loads = [
        pltpu.make_async_copy(src, dst, load_sem.at[k])
        for k, (src, dst) in enumerate(
            (
                (log_hbm, logbuf),
                (step_hbm, stepbuf),
                (skip_hbm, skip_ref),
                (convbc_hbm, convbc_ref),
                (convx_hbm, convx_ref),
                *[
                    (gain_hbm.at[:, pl.ds(k * LANES, LANES)], gain_ref.at[k])
                    for k in range(groups * TILES)
                ],
            )
        )
    ]
    at_bc = len(small_loads)
    bc_loads = [
        pltpu.make_async_copy(
            bc_hbm.at[:, pl.ds(k * LANES, LANES)], bcbuf.at[k, pl.ds(HALO, length)], load_sem.at[at_bc + k]
        )
        for k in range(2)
    ]

    def x_load(k):
        col = pl.ds(pl.multiple_of(k * LANES, LANES), LANES)
        return pltpu.make_async_copy(x_hbm.at[:, col], xbuf.at[k, pl.ds(HALO, length)], load_sem.at[at_bc + 2 + k])

    def z_load(k):
        col = pl.ds(pl.multiple_of(k * LANES, LANES), LANES)
        return pltpu.make_async_copy(
            z_hbm.at[:, col], zbuf.at[k], load_sem.at[at_bc + 2 + groups * TILES + k]
        )

    for load in small_loads + bc_loads:
        load.start()
    for k in range(groups * TILES):
        x_load(k).start()
    for k in range(groups * TILES):
        z_load(k).start()

    barrier = pltpu.get_barrier_semaphore()

    def greet_ctx(k):
        pl.semaphore_signal(barrier, inc=1, device_id=(lax.rem(me + ctx_size - k, ctx_size), tp), device_id_type=MESH)

    def greet_tp(k):
        pl.semaphore_signal(barrier, inc=1, device_id=(me, lax.rem(tp + k, tp_size)), device_id_type=MESH)

    for k in range(1, ctx_size):
        greet_ctx(k)
    for k in range(1, tp_size):
        greet_tp(k)

    right = lax.rem(me + 1, ctx_size)

    def halo_copy(src, dst, at):
        return pltpu.make_async_remote_copy(
            src_ref=src.at[pl.ds(length - HALO, HALO)], dst_ref=dst, send_sem=halo_send.at[at],
            recv_sem=halo_recv.at[at], device_id=(right, tp), device_id_type=MESH,
        )

    halos = [halo_copy(bc_hbm, bc_rim, 0), halo_copy(x_hbm, x_rim, 1)]
    s_at = lax.broadcasted_iota(jnp.int32, (CHUNK, CHUNK), 0)
    t_at = lax.broadcasted_iota(jnp.int32, (CHUNK, CHUNK), 1)
    upto = jnp.where(s_at <= t_at, 1.0, 0.0)
    sums[0] = (upto - jnp.where(s_at <= mid, 1.0, 0.0)).astype(BF16)
    sums[1] = upto.astype(BF16)
    sums[2] = jnp.ones((CHUNK, CHUNK), BF16)

    head_at = lax.broadcasted_iota(jnp.int32, (heads, channels), 0)
    channel_at = lax.broadcasted_iota(jnp.int32, (heads, channels), 1)
    first = head_at * head_dim
    one_map = jnp.where((channel_at >= first) & (channel_at < first + head_dim), 1.0, 0.0).astype(BF16)
    factor_map[...] = jnp.zeros_like(factor_map)
    for k in range(3):
        spread[k * heads : (k + 1) * heads, :] = one_map
        for term in range(2):
            row = (2 * k + term) * heads
            for lane in range(groups * TILES):
                factor_map[k, lane, row : row + heads, :] = one_map[:, lane * LANES : (lane + 1) * LANES]

    def shift(by, width, before):
        to = lax.broadcasted_iota(jnp.int32, (CHUNK, width), 0)
        at = lax.broadcasted_iota(jnp.int32, (CHUNK, width), 1)
        return jnp.where(to + (before - by) == at, 1.0, 0.0).astype(BF16)

    for by in range(1, 4):
        shift_all[by - 1] = shift(by, CHUNK, 0)
        shift_one[(by - 1) * CHUNK : by * CHUNK, :] = shift(by, CHUNK + HALO, HALO)
    halo_to = lax.broadcasted_iota(jnp.int32, (CHUNK, 3 * HALO), 0)
    halo_at = lax.broadcasted_iota(jnp.int32, (CHUNK, 3 * HALO), 1)
    halo_hit = halo_to < 0
    for by in range(1, 4):
        inside = (halo_at >= (by - 1) * HALO) & (halo_at < by * HALO)
        halo_hit = halo_hit | ((halo_to + (by * HALO - by) == halo_at) & inside)
    shift_rim[...] = jnp.where(halo_hit, 1.0, 0.0).astype(BF16)

    for load in small_loads:
        load.wait()

    def decays(b, carry):
        before, windows = carry
        batch = [b * BATCH + k for k in range(BATCH)]
        window = lax.broadcasted_iota(jnp.int32, (CHUNK, CHUNK), 1) * CHUNK + mid
        results = []
        for c in batch:
            pieces = jnp.concatenate(split3(logbuf[:, rows_of(c)]), axis=0)
            token = lax.broadcasted_iota(jnp.int32, (CHUNK, CHUNK), 0) + c * CHUNK
            hit = ((token <= window) & (token > window - CHUNK)) | (window == 15 * CHUNK + mid)
            matrix = jnp.concatenate((sums[0], sums[1], sums[2], jnp.where(hit, 1.0, 0.0).astype(BF16)), axis=1)
            result = dot(pieces, matrix)
            results.append(result[:heads] + result[heads : 2 * heads] + result[2 * heads :])
        for c, result in zip(batch, results):
            centred = result[:, :CHUNK]
            values = []
            for value in (
                jnp.exp(-centred) * stepbuf[:, rows_of(c)],
                jnp.exp(centred),
                jnp.exp(before + result[:, CHUNK : 2 * CHUNK]),
            ):
                high = value.astype(BF16).astype(F32)
                values += [high, value - high]
            factors[c] = jnp.concatenate(values, axis=0).T.astype(BF16)
            before = before + result[:, 2 * CHUNK : 3 * CHUNK]
            windows = windows + result[:, 3 * CHUNK :]
        return before, windows

    none = jnp.zeros((heads, CHUNK), F32)
    _, windows = lax.fori_loop(0, chunks // BATCH, decays, (none, none), unroll=True)
    head_rows = jnp.exp(windows).T[:16]
    lam_row = jnp.concatenate(split3(head_rows[15:16]) + (jnp.zeros((1, LANES - 3 * heads), BF16),), axis=1)
    lam_tile = jnp.broadcast_to(lam_row.astype(F32), (part_rows, LANES)).astype(BF16)

    def put_lam(d, _):
        parts[d, TILES] = lam_tile
        return 0

    lax.fori_loop(0, ctx_size, put_lam, 0, unroll=4)
    row_at = lax.broadcasted_iota(jnp.int32, (16, heads), 0)
    head_rows = jnp.where(row_at == 14, skip_ref[...], head_rows)
    head_rows = dot(jnp.concatenate(split3(head_rows), axis=1), spread[...])
    for lane in range(groups * TILES):
        rows_ref[lane] = head_rows[:, lane * LANES : (lane + 1) * LANES]

    def part_copy(src, dst, to):
        return pltpu.make_async_remote_copy(
            src_ref=src, dst_ref=dst, send_sem=part_send.at[0], recv_sem=part_recv.at[0],
            device_id=(to, tp), device_id_type=MESH,
        )

    def start_copy(src, dst, to):
        return pltpu.make_async_remote_copy(
            src_ref=src, dst_ref=dst, send_sem=start_send.at[0], recv_sem=start_recv.at[mine],
            device_id=(to, tp), device_id_type=MESH,
        )

    def await_starts(g):
        def some(count):
            bytes_of = send.at[pl.ds(0, count)]
            pltpu.make_async_remote_copy(
                src_ref=bytes_of, dst_ref=bytes_of, send_sem=start_send.at[0], recv_sem=start_recv.at[g],
                device_id=(right, tp), device_id_type=MESH,
            ).wait_recv()

        pl.when(mine != g)(lambda: some(per_group))
        if per_group > 1:
            pl.when(mine == g)(lambda: some(per_group - 1))

    def ssq_copy(p, to):
        return pltpu.make_async_remote_copy(
            src_ref=ssq.at[p], dst_ref=ssq_recv.at[p, tp], send_sem=ssq_send.at[p],
            recv_sem=ssq_recv_sem.at[p], device_id=(me, to), device_id_type=MESH,
        )

    def all_ssq(p):
        others = ssq_recv.at[p, pl.ds(0, tp_size - 1)]
        return pltpu.make_async_remote_copy(
            src_ref=others, dst_ref=others, send_sem=ssq_send.at[p], recv_sem=ssq_recv_sem.at[p],
            device_id=(me, tp), device_id_type=MESH,
        )

    others = pl.ds(0, ctx_size - 1)
    all_parts = part_copy(parts.at[others], recv.at[others], right)

    for load in bc_loads:
        load.wait()

    bc_taps = [0.5 * convbc_ref[k : k + 1, :] for k in range(4)]

    def project(side, b):
        part = slice(side * n_state, (side + 1) * n_state)
        blocks = [
            bcbuf[side, pl.ds(pl.multiple_of((b * BATCH + k) * CHUNK, CHUNK), CHUNK + HALO)] for k in range(BATCH)
        ]
        moved = [dot(shift_one[...], block) for block in blocks]
        results = []
        for block, move in zip(blocks, moved):
            half = bc_taps[3][:, part] * block[HALO:].astype(F32)
            for by in range(1, 4):
                half = half + bc_taps[3 - by][:, part] * move[(by - 1) * CHUNK : by * CHUNK]
            results.append(silu_of_half(half).astype(BF16))
        return results

    def project_b(b):
        for k, value in enumerate(project(0, b)):
            bt[b * BATCH + k] = value.T

    def project_c(b, _):
        values = project(1, b)
        causal = lax.broadcasted_iota(jnp.int32, (CHUNK, CHUNK), 0) >= lax.broadcasted_iota(
            jnp.int32, (CHUNK, CHUNK), 1
        )
        scores = [dot(value, bt[b * BATCH + k]) for k, value in enumerate(values)]
        for k, value in enumerate(values):
            c_ref[b * BATCH + k] = value
            scores_ref[b * BATCH + k] = jnp.where(causal, scores[k], 0.0).astype(BF16)
        return 0

    batches = chunks // BATCH

    def project_step(k, _):
        project_b(batches - 1 - k)
        return 0

    lax.fori_loop(0, batches - 1, project_step, 0, unroll=True)

    def carry_through():
        all_parts.wait_recv()
        col = pl.multiple_of(mine * GROUP, GROUP)
        decay = recv[:, TILES].reshape(ctx_size * part_rows, LANES)[:, : 3 * heads]
        decay = dot(decay, spread[:, pl.ds(col, GROUP)])
        lam_wide[...] = decay.reshape(ctx_size, part_rows, GROUP)

        def step(d, running):
            for k in range(TILES):
                send[d, k] = running[:, k * LANES : (k + 1) * LANES].astype(BF16)
            arrived = jnp.concatenate([recv[d, k] for k in range(TILES)], axis=1)
            return lam_wide[d] * running + arrived.astype(F32)

        lax.fori_loop(0, ctx_size, step, jnp.zeros((part_rows, GROUP), F32), unroll=4)
        here = start_state.at[pl.ds(mine * TILES, TILES), pl.ds(my_row, part_rows)]
        start_state[pl.ds(mine * TILES, TILES), pl.ds(my_row, part_rows)] = send[me]

        for k in range(1, ctx_size):
            far_first = (k + ctx_size // 3) % (ctx_size - 1) + 1
            to = lax.rem(me + far_first, ctx_size)
            start_copy(send.at[to], here, to).start()

    def tap_sums(g, b):
        col = pl.ds(pl.multiple_of(g * GROUP, GROUP), GROUP)
        taps = [(0.5 * convx_ref[k : k + 1, col]).astype(BF16) for k in range(3)]
        shifts = jnp.concatenate([shift_all[by] for by in range(3)] + [shift_rim[...]], axis=1)

        def one(k):
            at = pl.multiple_of((b * BATCH + k) * CHUNK, CHUNK)
            block = wide(xbuf, g, pl.ds(at, CHUNK + HALO))
            terms = [block * taps[3 - by] for by in range(1, 4)]
            stacked = jnp.concatenate([term[HALO:] for term in terms] + [term[:HALO] for term in terms], axis=0)
            return dot(shifts, stacked) + 0.5 * convx_ref[3:4, col] * block[HALO:].astype(F32)

        return one

    def scale_batch(g, b, next_sums):
        factor = factors[pl.ds(b * BATCH, BATCH)].reshape(BATCH * CHUNK, 6 * heads)
        scales = dot(factor, wide(factor_map.at[0], g, slice(None)))
        scaled = []
        for k in range(BATCH):
            value = silu_of_half(ahead[k])
            if next_sums is not None:
                ahead[k] = next_sums(k)
            put(xconv, g, (rows_of(b * BATCH + k),), value.astype(BF16))
            scaled.append((value * scales[k * CHUNK : (k + 1) * CHUNK]).astype(BF16))
            put(xs, g, (b * BATCH + k, slice(0, CHUNK)), scaled[-1])
        return scaled

    def leave(g):
        for r in range(per_group):
            for k in range(TILES):
                parts[carrier(g, r), k] = state[
                    r * part_rows : (r + 1) * part_rows, k * LANES : (k + 1) * LANES
                ].astype(BF16)

        def send_part(k):
            to = carrier(g, lax.rem(me // groups + k, per_group))
            part_copy(parts.at[to], recv.at[me], to).start()

        @pl.when(mine == g)
        def _():
            recv[me] = parts[me]

        @pl.when(mine != g)
        def _():
            send_part(0)

        for k in range(1, per_group):
            send_part(k)

    later = batches - 1
    count = groups * later

    def later_at(u):
        return lax.div(u, later), lax.rem(u, later) + 1

    def forward(u, _):
        scale_batch(*later_at(u), tap_sums(*later_at(lax.rem(u + 1, count))))
        return 0

    for k in range(groups * TILES):
        x_load(k).wait()
    first_sums = tap_sums(*later_at(jnp.int32(0)))
    for k in range(BATCH):
        ahead[k] = first_sums(k)
    lax.fori_loop(0, count // 2, forward, 0, unroll=2)
    pl.semaphore_wait(barrier, ctx_size + tp_size - 2)
    for halo in halos:
        halo.start()
    lax.fori_loop(count // 2, count, forward, 0, unroll=2)

    for halo, rim, ref in zip(halos, (bc_rim, x_rim), (bcbuf, xbuf)):
        halo.wait_recv()
        for k in range(ref.shape[0]):
            before = rim[:, k * LANES : (k + 1) * LANES].astype(F32)
            ref[k, 0:HALO] = jnp.where(me > 0, before, 0.0).astype(BF16)
    project_b(0)
    first_sums = tap_sums(jnp.int32(0), 0)
    for k in range(BATCH):
        ahead[k] = first_sums(k)

    def settle(g):
        scaled = scale_batch(g, 0, tap_sums(g + 1, 0) if g + 1 < groups else None)
        held = jnp.zeros((n_state, GROUP), F32)
        for c in range(chunks):
            value = scaled[c] if c < BATCH else wide(xs, g, c, slice(0, CHUNK))
            more = dot(bt[c], value)
            put(xs, g, (c, slice(CHUNK, CHUNK + n_state)), held.astype(BF16))
            held = wide(rows_ref, g, slice(c + 1, c + 2)) * (held + more)
        state[...] = held
        leave(jnp.int32(g))

    for g in range(groups):
        settle(g)

    lax.fori_loop(0, batches, project_c, 0)
    for k in range(groups * TILES):
        z_load(k).wait()

    def local(b, _):
        batch = [b * PAIR + k for k in range(PAIR)]
        factor = factors[pl.ds(b * PAIR, PAIR)].reshape(PAIR * CHUNK, 6 * heads)
        for g in range(groups):
            inner = [
                dot(
                    jnp.concatenate((scores_ref[c], c_ref[c]), axis=1),
                    wide(xs, g, c),
                )
                for c in batch
            ]
            scales = dot(factor, wide(factor_map.at[1], g, slice(None)))
            reaches = dot(factor, wide(factor_map.at[2], g, slice(None)))
            skip = wide(rows_ref, g, slice(14, 15))
            for k, c in enumerate(batch):
                part = slice(k * CHUNK, (k + 1) * CHUNK)
                gate = silu_of_half((wide(zbuf, g, rows_of(c)) * 0.5).astype(F32))
                skipped = skip * wide(xconv, g, rows_of(c)).astype(F32)
                put(local_ref, g, (rows_of(c),), (inner[k] * scales[part] + skipped) * gate)
                put(gate_ref, g, (rows_of(c),), (reaches[part] * gate).astype(BF16))
        return 0

    def local_step(b, _):
        pl.when(b == lax.min(1 + mine, chunks // PAIR - 1))(carry_through)
        return local(b, 0)

    lax.fori_loop(0, chunks // PAIR, local_step, 0)

    def finish(p, g):
        batch = [p * BATCH + k for k in range(BATCH)]
        c_rows = c_ref[pl.ds(p * BATCH, BATCH)].reshape(BATCH * CHUNK, n_state)
        carried = dot(c_rows, wide(start_state, g, slice(None)))
        gain = wide(gain_ref, g)
        totals = []
        for k, c in enumerate(batch):
            reach = wide(gate_ref, g, rows_of(c)).astype(F32)
            gated = wide(local_ref, g, rows_of(c)) + reach * carried[k * CHUNK : (k + 1) * CHUNK]
            put(local_ref, g, (rows_of(c),), gated * gain)
            both = gated * gated
            total = both[:, :LANES]
            for lane in range(LANES, GROUP, LANES):
                total = total + both[:, lane : lane + LANES]
            totals.append(total)
        return batch, totals

    def finish_group(g, _):
        await_starts(g)

        def step(p, _):
            for c, total in zip(*finish(p, g)):
                squares[c] = jnp.where(g == 0, 0.0, squares[c]) + total
            return 0

        lax.fori_loop(0, batches, step, 0)
        return 0

    lax.fori_loop(0, groups - 1, finish_group, 0)
    await_starts(groups - 1)

    def piece(p, _):
        for k, (c, total) in enumerate(zip(*finish(p, groups - 1))):
            ssq[p, k : k + 1, :] = jnp.sum((squares[c] + total).T, axis=0, keepdims=True)
        ssq[p, BATCH:, :] = jnp.zeros((8 - BATCH, LANES), F32)
        ssq_recv[p, tp] = ssq[p]
        for k in range(1, tp_size):
            ssq_copy(p, lax.rem(tp + (k + 1) % (tp_size - 1) + 1, tp_size)).start()
        return 0

    lax.fori_loop(0, batches, piece, 0, unroll=True)

    for halo in halos:
        halo.wait_send()
    all_parts.wait_send()
    start_copy(send.at[others], send.at[others], right).wait_send()

    def norm(b, _):
        all_ssq(b).wait_recv()
        mean = jnp.sum(ssq_recv[b], axis=0) * (1.0 / (channels * tp_size))
        inverse = lax.rsqrt(mean + 1e-5)
        for k in range(BATCH):
            at = rows_of(b * BATCH + k)
            column = jnp.broadcast_to(inverse[k : k + 1], (CHUNK, CHUNK)).T
            for lane in range(groups * TILES):
                here = slice(lane * LANES, (lane + 1) * LANES)
                out_ref[at, here] = (local_ref[lane, at] * column).astype(BF16)
        return 0

    lax.fori_loop(0, batches, norm, 0)
    for b in range(batches):
        all_ssq(b).wait_send()


def per_device(
    x_raw, bc_raw, z_gate, conv_x, conv_bc, step_size, log_decay, skip_scale, norm_gain, *, ctx_size, tp_size
):
    length, channels = x_raw.shape
    heads = step_size.shape[1]
    head_dim = channels // heads
    n_state = bc_raw.shape[1] // 2
    chunks = length // CHUNK
    groups = channels // GROUP
    lanes = channels // LANES
    part_rows = n_state * groups // ctx_size
    in_hbm = pl.BlockSpec(memory_space=pltpu.HBM)
    vmem = pltpu.VMEM
    dma = pltpu.SemaphoreType.DMA
    return pl.pallas_call(
        functools.partial(mixer, ctx_size, tp_size, head_dim),
        out_shape=pltpu.VMEM((length, channels), BF16),
        in_specs=[in_hbm] * 9,
        out_specs=pl.BlockSpec(memory_space=pltpu.VMEM),
        scratch_shapes=[
            vmem((lanes, length + HALO, LANES), BF16),
            vmem((2, length + HALO, n_state), BF16),
            vmem((lanes, length, LANES), BF16),
            vmem((HALO, channels), BF16),
            vmem((HALO, 2 * n_state), BF16),
            vmem((heads, length), F32),
            vmem((heads, length), F32),
            vmem((4, channels), F32),
            vmem((4, 2 * n_state), F32),
            vmem((1, heads), F32),
            vmem((lanes, 1, LANES), F32),
            vmem((3 * heads, channels), BF16),
            vmem((3, lanes, 6 * heads, LANES), BF16),
            vmem((3 * CHUNK, CHUNK + HALO), BF16),
            vmem((3, CHUNK, CHUNK), BF16),
            vmem((CHUNK, 3 * HALO), BF16),
            vmem((3, CHUNK, CHUNK), BF16),
            vmem((chunks, CHUNK, 6 * heads), BF16),
            vmem((lanes, 16, LANES), F32),
            vmem((chunks, CHUNK, CHUNK), BF16),
            vmem((chunks, CHUNK, n_state), BF16),
            vmem((chunks, n_state, CHUNK), BF16),
            vmem((lanes, length, LANES), BF16),
            vmem((lanes, chunks, CHUNK + n_state, LANES), BF16),
            vmem((n_state, GROUP), F32),
            vmem((ctx_size, TILES + 1, part_rows, LANES), BF16),
            vmem((ctx_size, TILES + 1, part_rows, LANES), BF16),
            vmem((ctx_size, part_rows, GROUP), F32),
            vmem((ctx_size, TILES, part_rows, LANES), BF16),
            vmem((lanes, n_state, LANES), BF16),
            vmem((BATCH, CHUNK, GROUP), F32),
            vmem((lanes, length, LANES), F32),
            vmem((lanes, length, LANES), BF16),
            vmem((chunks, CHUNK, LANES), F32),
            vmem((chunks // BATCH, 8, LANES), F32),
            vmem((chunks // BATCH, tp_size, 8, LANES), F32),
            dma((7 + 3 * lanes,)),
            dma((2,)),
            dma((2,)),
            dma((1,)),
            dma((1,)),
            dma((1,)),
            dma((groups,)),
            dma((chunks // BATCH,)),
            dma((chunks // BATCH,)),
        ],
        compiler_params=pltpu.CompilerParams(
            collective_id=0, has_side_effects=True, vmem_limit_bytes=56 * 1024 * 1024
        ),
        name="mixer",
    )(
        x_raw, bc_raw, z_gate, conv_x, conv_bc, step_size.T, log_decay.T,
        skip_scale.reshape(1, heads), norm_gain.reshape(1, channels),
    )


def solution(mesh):
    sizes = dict(mesh.shape)
    return jax.shard_map(
        functools.partial(per_device, ctx_size=sizes["ctx"], tp_size=sizes["tp"]),
        mesh=mesh,
        in_specs=(
            P("ctx", "tp"),
            P("ctx", None),
            P("ctx", "tp"),
            P(None, "tp"),
            P(),
            P("ctx", "tp"),
            P("ctx", "tp"),
            P("tp"),
            P("tp"),
        ),
        out_specs=P("ctx", "tp"),
        check_vma=False,
    )
```

```python
import functools

import jax
import jax.numpy as jnp
from jax import lax
from jax.experimental import pallas as pl
from jax.experimental.pallas import tpu as pltpu
from jax.sharding import PartitionSpec as P

F32 = jnp.float32
BF16 = jnp.bfloat16
MESH = pl.DeviceIdType.MESH
CHUNK = 128
LANES = 128
GROUP = 256
TILES = GROUP // LANES
HALO = 16
BATCH = 4
PAIR = 2


def split3(value):
    high = value.astype(BF16)
    rest = value - high.astype(F32)
    mid = rest.astype(BF16)
    return high, mid, (rest - mid.astype(F32)).astype(BF16)


def silu_of_half(half):
    return half * jnp.tanh(half) + half


def dot(left, right):
    return jnp.dot(left, right, preferred_element_type=F32)


def each_other(size, fn):
    count = size - 1
    unroll = next(n for n in (6, 5, 4, 3, 2, 1) if (count - 1) % n == 0)

    def step(k, _):
        fn(k)
        return 0

    if count > 1:
        lax.fori_loop(1, count, step, 0, unroll=unroll)
    fn(count)


def mixer(
    ctx_size, tp_size, head_dim,
    x_hbm, bc_hbm, z_hbm, convx_hbm, convbc_hbm, step_hbm, log_hbm, skip_hbm, gain_hbm,
    out_ref,
    xbuf, bcbuf, zbuf, x_rim, bc_rim, stepbuf, logbuf, convx_ref, convbc_ref, skip_ref, gain_ref,
    spread, factor_map, shift_one, shift_all, shift_rim, sums, factors, rows_ref,
    scores_ref, c_ref, bt, xconv, xs, state, parts, recv, lam_wide, send, start_state,
    ahead, local_ref, gate_ref, squares, ssq, ssq_recv,
    load_sem, halo_send, halo_recv, part_send, part_recv, start_send, start_recv, ssq_send, ssq_recv_sem,
):
    length, channels = x_hbm.shape
    heads = step_hbm.shape[0]
    chunks = length // CHUNK
    groups = channels // GROUP
    n_state = bt.shape[1]
    part_rows = parts.shape[2]
    per_group = ctx_size // groups
    mid = CHUNK // 2 - 1
    me = lax.axis_index("ctx")
    tp = lax.axis_index("tp")
    mine = lax.rem(me // 2 + me // 8, 2) * 2 + lax.rem(me, 2)
    my_row = pl.multiple_of((me // groups) * part_rows, part_rows)

    def carrier(g, r):
        return r * groups + lax.rem(g // 2 + r // 2, 2) * 2 + lax.rem(g, 2)

    def wide(ref, g, *at):
        return jnp.concatenate([ref[(g * TILES + k, *at)] if at else ref[g * TILES + k] for k in range(TILES)], axis=-1)

    def put(ref, g, at, value):
        for k in range(TILES):
            ref[(g * TILES + k, *at)] = value[:, k * LANES : (k + 1) * LANES]

    def rows_of(c):
        return pl.ds(pl.multiple_of(c * CHUNK, CHUNK), CHUNK)

    small_loads = [
        pltpu.make_async_copy(src, dst, load_sem.at[k])
        for k, (src, dst) in enumerate(
            (
                (log_hbm, logbuf),
                (step_hbm, stepbuf),
                (skip_hbm, skip_ref),
                (convbc_hbm, convbc_ref),
                (convx_hbm, convx_ref),
                *[
                    (gain_hbm.at[:, pl.ds(k * LANES, LANES)], gain_ref.at[k])
                    for k in range(groups * TILES)
                ],
            )
        )
    ]
    at_bc = len(small_loads)
    bc_loads = [
        pltpu.make_async_copy(
            bc_hbm.at[:, pl.ds(k * LANES, LANES)], bcbuf.at[k, pl.ds(HALO, length)], load_sem.at[at_bc + k]
        )
        for k in range(2)
    ]

    def x_load(k):
        col = pl.ds(pl.multiple_of(k * LANES, LANES), LANES)
        return pltpu.make_async_copy(x_hbm.at[:, col], xbuf.at[k, pl.ds(HALO, length)], load_sem.at[at_bc + 2 + k])

    def z_load(k):
        col = pl.ds(pl.multiple_of(k * LANES, LANES), LANES)
        return pltpu.make_async_copy(
            z_hbm.at[:, col], zbuf.at[k], load_sem.at[at_bc + 2 + groups * TILES + k]
        )

    for load in small_loads + bc_loads:
        load.start()
    for k in range(groups * TILES):
        x_load(k).start()
    for k in range(groups * TILES):
        z_load(k).start()

    barrier = pltpu.get_barrier_semaphore()

    def greet_ctx(k):
        pl.semaphore_signal(barrier, inc=1, device_id=(lax.rem(me + ctx_size - k, ctx_size), tp), device_id_type=MESH)

    def greet_tp(k):
        pl.semaphore_signal(barrier, inc=1, device_id=(me, lax.rem(tp + k, tp_size)), device_id_type=MESH)

    each_other(ctx_size, greet_ctx)
    each_other(tp_size, greet_tp)

    right = lax.rem(me + 1, ctx_size)

    def halo_copy(src, dst, at):
        return pltpu.make_async_remote_copy(
            src_ref=src.at[pl.ds(length - HALO, HALO)], dst_ref=dst, send_sem=halo_send.at[at],
            recv_sem=halo_recv.at[at], device_id=(right, tp), device_id_type=MESH,
        )

    halos = [halo_copy(bc_hbm, bc_rim, 0), halo_copy(x_hbm, x_rim, 1)]
    s_at = lax.broadcasted_iota(jnp.int32, (CHUNK, CHUNK), 0)
    t_at = lax.broadcasted_iota(jnp.int32, (CHUNK, CHUNK), 1)
    upto = jnp.where(s_at <= t_at, 1.0, 0.0)
    sums[0] = (upto - jnp.where(s_at <= mid, 1.0, 0.0)).astype(BF16)
    sums[1] = upto.astype(BF16)
    sums[2] = jnp.ones((CHUNK, CHUNK), BF16)

    head_at = lax.broadcasted_iota(jnp.int32, (heads, channels), 0)
    channel_at = lax.broadcasted_iota(jnp.int32, (heads, channels), 1)
    first = head_at * head_dim
    one_map = jnp.where((channel_at >= first) & (channel_at < first + head_dim), 1.0, 0.0).astype(BF16)
    factor_map[...] = jnp.zeros_like(factor_map)
    for k in range(3):
        spread[k * heads : (k + 1) * heads, :] = one_map
        for term in range(2):
            row = (2 * k + term) * heads
            for lane in range(groups * TILES):
                factor_map[k, lane, row : row + heads, :] = one_map[:, lane * LANES : (lane + 1) * LANES]

    def shift(by, width, before):
        to = lax.broadcasted_iota(jnp.int32, (CHUNK, width), 0)
        at = lax.broadcasted_iota(jnp.int32, (CHUNK, width), 1)
        return jnp.where(to + (before - by) == at, 1.0, 0.0).astype(BF16)

    for by in range(1, 4):
        shift_all[by - 1] = shift(by, CHUNK, 0)
        shift_one[(by - 1) * CHUNK : by * CHUNK, :] = shift(by, CHUNK + HALO, HALO)
    halo_to = lax.broadcasted_iota(jnp.int32, (CHUNK, 3 * HALO), 0)
    halo_at = lax.broadcasted_iota(jnp.int32, (CHUNK, 3 * HALO), 1)
    halo_hit = halo_to < 0
    for by in range(1, 4):
        inside = (halo_at >= (by - 1) * HALO) & (halo_at < by * HALO)
        halo_hit = halo_hit | ((halo_to + (by * HALO - by) == halo_at) & inside)
    shift_rim[...] = jnp.where(halo_hit, 1.0, 0.0).astype(BF16)

    for load in small_loads:
        load.wait()

    def decays(b, carry):
        before, windows = carry
        batch = [b * BATCH + k for k in range(BATCH)]
        window = lax.broadcasted_iota(jnp.int32, (CHUNK, CHUNK), 1) * CHUNK + mid
        results = []
        for c in batch:
            pieces = jnp.concatenate(split3(logbuf[:, rows_of(c)]), axis=0)
            token = lax.broadcasted_iota(jnp.int32, (CHUNK, CHUNK), 0) + c * CHUNK
            hit = ((token <= window) & (token > window - CHUNK)) | (window == 15 * CHUNK + mid)
            matrix = jnp.concatenate((sums[0], sums[1], sums[2], jnp.where(hit, 1.0, 0.0).astype(BF16)), axis=1)
            result = dot(pieces, matrix)
            results.append(result[:heads] + result[heads : 2 * heads] + result[2 * heads :])
        for c, result in zip(batch, results):
            centred = result[:, :CHUNK]
            values = []
            for value in (
                jnp.exp(-centred) * stepbuf[:, rows_of(c)],
                jnp.exp(centred),
                jnp.exp(before + result[:, CHUNK : 2 * CHUNK]),
            ):
                high = value.astype(BF16).astype(F32)
                values += [high, value - high]
            factors[c] = jnp.concatenate(values, axis=0).T.astype(BF16)
            before = before + result[:, 2 * CHUNK : 3 * CHUNK]
            windows = windows + result[:, 3 * CHUNK :]
        return before, windows

    none = jnp.zeros((heads, CHUNK), F32)
    _, windows = lax.fori_loop(0, chunks // BATCH, decays, (none, none), unroll=True)
    head_rows = jnp.exp(windows).T[:16]
    lam_row = jnp.concatenate(split3(head_rows[15:16]) + (jnp.zeros((1, LANES - 3 * heads), BF16),), axis=1)
    lam_tile = jnp.broadcast_to(lam_row.astype(F32), (part_rows, LANES)).astype(BF16)

    def put_lam(d, _):
        parts[d, TILES] = lam_tile
        return 0

    lax.fori_loop(0, ctx_size, put_lam, 0, unroll=4)
    row_at = lax.broadcasted_iota(jnp.int32, (16, heads), 0)
    head_rows = jnp.where(row_at == 14, skip_ref[...], head_rows)
    head_rows = dot(jnp.concatenate(split3(head_rows), axis=1), spread[...])
    for lane in range(groups * TILES):
        rows_ref[lane] = head_rows[:, lane * LANES : (lane + 1) * LANES]

    def part_copy(src, dst, to):
        return pltpu.make_async_remote_copy(
            src_ref=src, dst_ref=dst, send_sem=part_send.at[0], recv_sem=part_recv.at[0],
            device_id=(to, tp), device_id_type=MESH,
        )

    def start_copy(src, dst, to):
        return pltpu.make_async_remote_copy(
            src_ref=src, dst_ref=dst, send_sem=start_send.at[0], recv_sem=start_recv.at[mine],
            device_id=(to, tp), device_id_type=MESH,
        )

    def await_starts(g):
        def some(count):
            bytes_of = send.at[pl.ds(0, count)]
            pltpu.make_async_remote_copy(
                src_ref=bytes_of, dst_ref=bytes_of, send_sem=start_send.at[0], recv_sem=start_recv.at[g],
                device_id=(right, tp), device_id_type=MESH,
            ).wait_recv()

        pl.when(mine != g)(lambda: some(per_group))
        if per_group > 1:
            pl.when(mine == g)(lambda: some(per_group - 1))

    def ssq_copy(p, to):
        return pltpu.make_async_remote_copy(
            src_ref=ssq.at[p], dst_ref=ssq_recv.at[p, tp], send_sem=ssq_send.at[p],
            recv_sem=ssq_recv_sem.at[p], device_id=(me, to), device_id_type=MESH,
        )

    def all_ssq(p):
        others = ssq_recv.at[p, pl.ds(0, tp_size - 1)]
        return pltpu.make_async_remote_copy(
            src_ref=others, dst_ref=others, send_sem=ssq_send.at[p], recv_sem=ssq_recv_sem.at[p],
            device_id=(me, tp), device_id_type=MESH,
        )

    others = pl.ds(0, ctx_size - 1)
    all_parts = part_copy(parts.at[others], recv.at[others], right)

    for load in bc_loads:
        load.wait()

    bc_taps = [0.5 * convbc_ref[k : k + 1, :] for k in range(4)]

    def project(side, b):
        part = slice(side * n_state, (side + 1) * n_state)
        blocks = [
            bcbuf[side, pl.ds(pl.multiple_of((b * BATCH + k) * CHUNK, CHUNK), CHUNK + HALO)] for k in range(BATCH)
        ]
        moved = [dot(shift_one[...], block) for block in blocks]
        results = []
        for block, move in zip(blocks, moved):
            half = bc_taps[3][:, part] * block[HALO:].astype(F32)
            for by in range(1, 4):
                half = half + bc_taps[3 - by][:, part] * move[(by - 1) * CHUNK : by * CHUNK]
            results.append(silu_of_half(half).astype(BF16))
        return results

    def project_b(b):
        for k, value in enumerate(project(0, b)):
            bt[b * BATCH + k] = value.T

    def project_c(b, _):
        values = project(1, b)
        causal = lax.broadcasted_iota(jnp.int32, (CHUNK, CHUNK), 0) >= lax.broadcasted_iota(
            jnp.int32, (CHUNK, CHUNK), 1
        )
        scores = [dot(value, bt[b * BATCH + k]) for k, value in enumerate(values)]
        for k, value in enumerate(values):
            c_ref[b * BATCH + k] = value
            scores_ref[b * BATCH + k] = jnp.where(causal, scores[k], 0.0).astype(BF16)
        return 0

    batches = chunks // BATCH

    def project_step(k, _):
        project_b(batches - 1 - k)
        return 0

    lax.fori_loop(0, batches - 1, project_step, 0, unroll=True)

    def carry_through():
        all_parts.wait_recv()
        col = pl.multiple_of(mine * GROUP, GROUP)
        decay = recv[:, TILES].reshape(ctx_size * part_rows, LANES)[:, : 3 * heads]
        decay = dot(decay, spread[:, pl.ds(col, GROUP)])
        lam_wide[...] = decay.reshape(ctx_size, part_rows, GROUP)

        def step(d, running):
            for k in range(TILES):
                send[d, k] = running[:, k * LANES : (k + 1) * LANES].astype(BF16)
            arrived = jnp.concatenate([recv[d, k] for k in range(TILES)], axis=1)
            return lam_wide[d] * running + arrived.astype(F32)

        lax.fori_loop(0, ctx_size, step, jnp.zeros((part_rows, GROUP), F32), unroll=4)
        here = start_state.at[pl.ds(mine * TILES, TILES), pl.ds(my_row, part_rows)]
        start_state[pl.ds(mine * TILES, TILES), pl.ds(my_row, part_rows)] = send[me]

        def send_start(k):
            far_first = lax.rem(k + ctx_size // 3, ctx_size - 1) + 1
            to = lax.rem(me + far_first, ctx_size)
            start_copy(send.at[to], here, to).start()

        each_other(ctx_size, send_start)

    def tap_sums(g, b):
        col = pl.ds(pl.multiple_of(g * GROUP, GROUP), GROUP)
        taps = [(0.5 * convx_ref[k : k + 1, col]).astype(BF16) for k in range(3)]
        shifts = jnp.concatenate([shift_all[by] for by in range(3)] + [shift_rim[...]], axis=1)

        def one(k):
            at = pl.multiple_of((b * BATCH + k) * CHUNK, CHUNK)
            block = wide(xbuf, g, pl.ds(at, CHUNK + HALO))
            terms = [block * taps[3 - by] for by in range(1, 4)]
            stacked = jnp.concatenate([term[HALO:] for term in terms] + [term[:HALO] for term in terms], axis=0)
            return dot(shifts, stacked) + 0.5 * convx_ref[3:4, col] * block[HALO:].astype(F32)

        return one

    def scale_batch(g, b, next_sums):
        factor = factors[pl.ds(b * BATCH, BATCH)].reshape(BATCH * CHUNK, 6 * heads)
        scales = dot(factor, wide(factor_map.at[0], g, slice(None)))
        scaled = []
        for k in range(BATCH):
            value = silu_of_half(ahead[k])
            ahead[k] = next_sums(k)
            put(xconv, g, (rows_of(b * BATCH + k),), value.astype(BF16))
            scaled.append((value * scales[k * CHUNK : (k + 1) * CHUNK]).astype(BF16))
            put(xs, g, (b * BATCH + k, slice(0, CHUNK)), scaled[-1])
        return scaled

    def leave(g):
        for r in range(per_group):
            for k in range(TILES):
                parts[carrier(g, r), k] = state[
                    r * part_rows : (r + 1) * part_rows, k * LANES : (k + 1) * LANES
                ].astype(BF16)

        def send_part(k):
            to = carrier(g, lax.rem(me // groups + k, per_group))
            part_copy(parts.at[to], recv.at[me], to).start()

        @pl.when(mine == g)
        def _():
            recv[me] = parts[me]

        @pl.when(mine != g)
        def _():
            send_part(0)

        if per_group > 1:
            each_other(per_group, send_part)

    later = batches - 1
    count = groups * later

    def later_at(u):
        return lax.div(u, later), lax.rem(u, later) + 1

    def forward(u, _):
        scale_batch(*later_at(u), tap_sums(*later_at(lax.rem(u + 1, count))))
        return 0

    for k in range(groups * TILES):
        x_load(k).wait()
    first_sums = tap_sums(*later_at(jnp.int32(0)))
    for k in range(BATCH):
        ahead[k] = first_sums(k)
    lax.fori_loop(0, count // 4, forward, 0, unroll=2)
    pl.semaphore_wait(barrier, ctx_size + tp_size - 2)
    for halo in halos:
        halo.start()
    lax.fori_loop(count // 4, count, forward, 0, unroll=2)

    for halo, rim, ref in zip(halos, (bc_rim, x_rim), (bcbuf, xbuf)):
        halo.wait_recv()
        for k in range(ref.shape[0]):
            before = rim[:, k * LANES : (k + 1) * LANES].astype(F32)
            ref[k, 0:HALO] = jnp.where(me > 0, before, 0.0).astype(BF16)
    project_b(0)
    first_sums = tap_sums(jnp.int32(0), 0)
    for k in range(BATCH):
        ahead[k] = first_sums(k)

    def settle(g, _):
        scaled = scale_batch(g, 0, tap_sums(lax.rem(g + 1, groups), 0))
        held = jnp.zeros((n_state, GROUP), F32)
        for c in range(chunks):
            value = scaled[c] if c < BATCH else wide(xs, g, c, slice(0, CHUNK))
            more = dot(bt[c], value)
            put(xs, g, (c, slice(CHUNK, CHUNK + n_state)), held.astype(BF16))
            held = wide(rows_ref, g, slice(c + 1, c + 2)) * (held + more)
        state[...] = held
        leave(g)
        return 0

    lax.fori_loop(0, groups, settle, 0)

    lax.fori_loop(0, batches, project_c, 0)
    for k in range(groups * TILES):
        z_load(k).wait()

    def local(b, _):
        batch = [b * PAIR + k for k in range(PAIR)]
        factor = factors[pl.ds(b * PAIR, PAIR)].reshape(PAIR * CHUNK, 6 * heads)
        for g in range(groups):
            inner = [
                dot(
                    jnp.concatenate((scores_ref[c], c_ref[c]), axis=1),
                    wide(xs, g, c),
                )
                for c in batch
            ]
            scales = dot(factor, wide(factor_map.at[1], g, slice(None)))
            reaches = dot(factor, wide(factor_map.at[2], g, slice(None)))
            skip = wide(rows_ref, g, slice(14, 15))
            for k, c in enumerate(batch):
                part = slice(k * CHUNK, (k + 1) * CHUNK)
                gate = silu_of_half((wide(zbuf, g, rows_of(c)) * 0.5).astype(F32))
                skipped = skip * wide(xconv, g, rows_of(c)).astype(F32)
                put(local_ref, g, (rows_of(c),), (inner[k] * scales[part] + skipped) * gate)
                put(gate_ref, g, (rows_of(c),), (reaches[part] * gate).astype(BF16))
        return 0

    def local_step(b, _):
        pl.when(b == lax.min(chunks // PAIR // 3 + mine, chunks // PAIR - 1))(carry_through)
        return local(b, 0)

    lax.fori_loop(0, chunks // PAIR, local_step, 0)

    def finish(p, g):
        batch = [p * BATCH + k for k in range(BATCH)]
        c_rows = c_ref[pl.ds(p * BATCH, BATCH)].reshape(BATCH * CHUNK, n_state)
        carried = dot(c_rows, wide(start_state, g, slice(None)))
        gain = wide(gain_ref, g)
        totals = []
        for k, c in enumerate(batch):
            reach = wide(gate_ref, g, rows_of(c)).astype(F32)
            gated = wide(local_ref, g, rows_of(c)) + reach * carried[k * CHUNK : (k + 1) * CHUNK]
            put(local_ref, g, (rows_of(c),), gated * gain)
            both = gated * gated
            total = both[:, :LANES]
            for lane in range(LANES, GROUP, LANES):
                total = total + both[:, lane : lane + LANES]
            totals.append(total)
        return batch, totals

    def finish_group(g, _):
        await_starts(g)

        def step(p, _):
            for c, total in zip(*finish(p, g)):
                squares[c] = jnp.where(g == 0, 0.0, squares[c]) + total
            return 0

        lax.fori_loop(0, batches, step, 0)
        return 0

    lax.fori_loop(0, groups - 1, finish_group, 0)
    await_starts(groups - 1)

    def piece(p, _):
        for k, (c, total) in enumerate(zip(*finish(p, groups - 1))):
            ssq[p, k : k + 1, :] = jnp.sum((squares[c] + total).T, axis=0, keepdims=True)
        ssq[p, BATCH:, :] = jnp.zeros((8 - BATCH, LANES), F32)
        ssq_recv[p, tp] = ssq[p]
        each_other(
            tp_size, lambda k: ssq_copy(p, lax.rem(tp + lax.rem(k + 1, tp_size - 1) + 1, tp_size)).start()
        )
        return 0

    lax.fori_loop(0, batches, piece, 0, unroll=True)

    for halo in halos:
        halo.wait_send()
    all_parts.wait_send()
    start_copy(send.at[others], send.at[others], right).wait_send()

    def norm(b, _):
        all_ssq(b).wait_recv()
        mean = jnp.sum(ssq_recv[b], axis=0) * (1.0 / (channels * tp_size))
        inverse = lax.rsqrt(mean + 1e-5)
        for k in range(BATCH):
            at = rows_of(b * BATCH + k)
            column = jnp.broadcast_to(inverse[k : k + 1], (CHUNK, CHUNK)).T
            for lane in range(groups * TILES):
                here = slice(lane * LANES, (lane + 1) * LANES)
                out_ref[at, here] = (local_ref[lane, at] * column).astype(BF16)
        return 0

    lax.fori_loop(0, batches, norm, 0)
    for b in range(batches):
        all_ssq(b).wait_send()


def per_device(
    x_raw, bc_raw, z_gate, conv_x, conv_bc, step_size, log_decay, skip_scale, norm_gain, *, ctx_size, tp_size
):
    length, channels = x_raw.shape
    heads = step_size.shape[1]
    head_dim = channels // heads
    n_state = bc_raw.shape[1] // 2
    chunks = length // CHUNK
    groups = channels // GROUP
    lanes = channels // LANES
    part_rows = n_state * groups // ctx_size
    in_hbm = pl.BlockSpec(memory_space=pltpu.HBM)
    vmem = pltpu.VMEM
    dma = pltpu.SemaphoreType.DMA
    return pl.pallas_call(
        functools.partial(mixer, ctx_size, tp_size, head_dim),
        out_shape=pltpu.VMEM((length, channels), BF16),
        in_specs=[in_hbm] * 9,
        out_specs=pl.BlockSpec(memory_space=pltpu.VMEM),
        scratch_shapes=[
            vmem((lanes, length + HALO, LANES), BF16),
            vmem((2, length + HALO, n_state), BF16),
            vmem((lanes, length, LANES), BF16),
            vmem((HALO, channels), BF16),
            vmem((HALO, 2 * n_state), BF16),
            vmem((heads, length), F32),
            vmem((heads, length), F32),
            vmem((4, channels), F32),
            vmem((4, 2 * n_state), F32),
            vmem((1, heads), F32),
            vmem((lanes, 1, LANES), F32),
            vmem((3 * heads, channels), BF16),
            vmem((3, lanes, 6 * heads, LANES), BF16),
            vmem((3 * CHUNK, CHUNK + HALO), BF16),
            vmem((3, CHUNK, CHUNK), BF16),
            vmem((CHUNK, 3 * HALO), BF16),
            vmem((3, CHUNK, CHUNK), BF16),
            vmem((chunks, CHUNK, 6 * heads), BF16),
            vmem((lanes, 16, LANES), F32),
            vmem((chunks, CHUNK, CHUNK), BF16),
            vmem((chunks, CHUNK, n_state), BF16),
            vmem((chunks, n_state, CHUNK), BF16),
            vmem((lanes, length, LANES), BF16),
            vmem((lanes, chunks, CHUNK + n_state, LANES), BF16),
            vmem((n_state, GROUP), F32),
            vmem((ctx_size, TILES + 1, part_rows, LANES), BF16),
            vmem((ctx_size, TILES + 1, part_rows, LANES), BF16),
            vmem((ctx_size, part_rows, GROUP), F32),
            vmem((ctx_size, TILES, part_rows, LANES), BF16),
            vmem((lanes, n_state, LANES), BF16),
            vmem((BATCH, CHUNK, GROUP), F32),
            vmem((lanes, length, LANES), F32),
            vmem((lanes, length, LANES), BF16),
            vmem((chunks, CHUNK, LANES), F32),
            vmem((chunks // BATCH, 8, LANES), F32),
            vmem((chunks // BATCH, tp_size, 8, LANES), F32),
            dma((7 + 3 * lanes,)),
            dma((2,)),
            dma((2,)),
            dma((1,)),
            dma((1,)),
            dma((1,)),
            dma((groups,)),
            dma((chunks // BATCH,)),
            dma((chunks // BATCH,)),
        ],
        compiler_params=pltpu.CompilerParams(
            collective_id=0, has_side_effects=True, vmem_limit_bytes=56 * 1024 * 1024
        ),
        name="mixer",
    )(
        x_raw, bc_raw, z_gate, conv_x, conv_bc, step_size.T, log_decay.T,
        skip_scale.reshape(1, heads), norm_gain.reshape(1, channels),
    )


def solution(mesh):
    sizes = dict(mesh.shape)
    return jax.shard_map(
        functools.partial(per_device, ctx_size=sizes["ctx"], tp_size=sizes["tp"]),
        mesh=mesh,
        in_specs=(
            P("ctx", "tp"),
            P("ctx", None),
            P("ctx", "tp"),
            P(None, "tp"),
            P(),
            P("ctx", "tp"),
            P("ctx", "tp"),
            P("tp"),
            P("tp"),
        ),
        out_specs=P("ctx", "tp"),
        check_vma=False,
    )
```
